256 devices in a mesh: seq: 16 (over x_hi, z), head: 16 (over y, x_lo, core).
Axes of the slice: x: 4 (x_hi: 2, x_lo: 2; x = x_hi * 2 + x_lo), y: 4, z: 8, core: 2. Of those that a mesh axis runs over, the one named last changes fastest.
Arguments:
- inputs: bfloat16 [32768, 4096], P('seq', 'head'), may hold values from -6 to 6
- bc_inputs: bfloat16 [32768, 256], P('seq'), may hold values from -6 to 6
- dt_raw: bfloat16 [64, 32768], P(None, 'seq'), may hold values from -2.5 to 2.5
- conv_inner: float32 [4, 4096], replicated, may hold values from -3 to 3
- conv_state: float32 [4, 256], replicated, may hold values from -3 to 3
- log_rate: float32 [64], replicated, may hold values from -2.78 to 1.61
- dt_bias: float32 [64], replicated, as said below
- skip_gain: float32 [64], replicated, may hold values from 0.5 to 2
Outputs:
- mixed: bfloat16 [32768, 4096], P('seq', 'head')
The draws below stay inside these ranges and needn't reach their ends.
Inputs may be any that keep to these rules, and one draw needn't show every extreme that they name: dt_bias lies between log(4 / 32768) - 0.3 and -4.
All inputs are finite; a program needn't handle non-finite values.
Results may differ from the reference program's by a relative error of at most 0.0034.
Values may be sent and summed in bfloat16 or wider, within the bound.
A program may use at most 128 MiB of HBM per device.

```python
import math
import jax
import jax.numpy as jnp
from jax import lax

DI = 4096
NH = 64
STATE = 128
TAPS = 4
BLOCK = 512
LENGTH = 32768


def head_pattern(key):
    chooser = jax.random.uniform(jax.random.fold_in(key, 11), (NH,))
    lasting = chooser < 0.5
    long_bias = jnp.log(4.0 / LENGTH) + jax.random.uniform(jax.random.fold_in(key, 12), (NH,), minval=-0.3, maxval=0.3)
    short_bias = jax.random.uniform(jax.random.fold_in(key, 13), (NH,), minval=-5.0, maxval=-4.0)
    long_rate = jax.random.uniform(jax.random.fold_in(key, 14), (NH,), minval=0.25, maxval=1.0) / 4.0
    short_rate = jax.random.uniform(jax.random.fold_in(key, 15), (NH,), minval=0.02, maxval=0.0333) / jnp.exp(short_bias)
    bias = jnp.where(lasting, long_bias, short_bias)
    log_value = jnp.log(jnp.where(lasting, long_rate, short_rate))
    return (bias.astype(jnp.float32), log_value.astype(jnp.float32))


def draw_dt_bias(key, part):
    return head_pattern(key)[0]


def draw_log_rate(key, part):
    return head_pattern(key)[1]


def levels(own_key, extent, split, low, largest):
    def one(position, parts):
        steps = jax.random.uniform(jax.random.fold_in(jax.random.fold_in(own_key, 6), position), (parts,), jnp.float32, low / len(split), largest / len(split))
        return jnp.repeat(jnp.exp(steps), extent[position] // parts).reshape((-1,) + (1,) * (len(extent) - position - 1))

    loudness = one(*split[0])
    for cut in split[1:]:
        loudness = loudness * one(*cut)
    return loudness


def noise(stream_key, extent, scale, most, cuts=(), held_as=jnp.bfloat16):
    level = levels(stream_key, extent, cuts, -0.22, 0.18) if cuts else 1.0
    drawn = jax.random.normal(stream_key, extent, jnp.float32) * scale * level
    return jnp.minimum(jnp.maximum(drawn, -most), most).astype(held_as)


def setup_inputs(seed: int = 0) -> dict:
    seeds = jax.random.split(jax.random.key(seed), 9)
    return {
        "inputs": noise(seeds[0], (LENGTH, DI), 1.0, 6.0, ((0, 16), (1, 16))),
        "bc_inputs": noise(seeds[1], (LENGTH, 2 * STATE), 1.0, 6.0, ((0, 16),)),
        "dt_raw": noise(seeds[2], (NH, LENGTH), 0.5, 2.5, ((1, 16),)),
        "conv_inner": noise(seeds[3], (TAPS, DI), TAPS ** -0.5, 3.0, (), jnp.float32),
        "conv_state": noise(seeds[4], (TAPS, 2 * STATE), TAPS ** -0.5, 3.0, (), jnp.float32),
        "log_rate": draw_log_rate(jax.random.fold_in(seeds[8], 71), 0),
        "dt_bias": draw_dt_bias(jax.random.fold_in(seeds[8], 71), 0),
        "skip_gain": jnp.clip(jnp.exp(jax.random.uniform(seeds[7], (NH,), jnp.float32, math.log(0.5), math.log(2.0))), 0.5, 2.0),
    }


HIGHEST = lax.Precision.HIGHEST


def conv_silu(sequence, weights):
    length_total = sequence.shape[0]
    tap_count = weights.shape[0]
    padded = jnp.pad(sequence, ((tap_count - 1, 0), (0, 0)))
    total = jnp.zeros(sequence.shape, jnp.float32)
    for tap_index in range(tap_count):
        total = total + weights[tap_index][None, :] * padded[tap_index:tap_index + length_total]
    return jax.nn.silu(total)


def block_scan(values, b_part, c_part, steps, rate):
    row_count = values.shape[0]
    head_count = steps.shape[0]
    head_width = values.shape[1] // head_count
    state_size = b_part.shape[1]
    block_count = row_count // BLOCK
    blocked_values = values.reshape(block_count, BLOCK, head_count, head_width)
    blocked_b = b_part.reshape(block_count, BLOCK, state_size)
    blocked_c = c_part.reshape(block_count, BLOCK, state_size)
    blocked_steps = steps.reshape(head_count, block_count, BLOCK).transpose(1, 0, 2)
    lower_mask = jnp.tril(jnp.ones((BLOCK, BLOCK), bool))

    def one_block(carry_pair, block_item):
        carry_state, offset = carry_pair
        value_block, b_block, c_block, step_block = block_item
        cumulative = jnp.cumsum(step_block * rate[:, None], axis=1)
        spread = jnp.where(lower_mask[None], cumulative[:, :, None] - cumulative[:, None, :], -jnp.inf)
        scores = jnp.dot(c_block, b_block.T, precision=HIGHEST)
        weights = scores[None] * jnp.exp(spread) * step_block[:, None, :]
        inner_part = jnp.einsum("hts,shp->thp", weights, value_block, precision=HIGHEST)
        carried = jnp.einsum("tn,hpn->thp", c_block, carry_state, precision=HIGHEST) * jnp.exp(cumulative).T[:, :, None]
        tail_weight = (jnp.exp(cumulative[:, -1:] - cumulative) * step_block).T
        update = jnp.einsum("shp,sn->hpn", value_block * tail_weight[:, :, None], b_block, precision=HIGHEST)
        carry_state = jnp.exp(cumulative[:, -1])[:, None, None] * carry_state + update
        return (carry_state, offset + cumulative[:, -1]), (inner_part + carried, offset[:, None] + cumulative)

    start_pair = (jnp.zeros((head_count, head_width, state_size), jnp.float32), jnp.zeros((head_count,), jnp.float32))
    final_pair, stacked = lax.scan(one_block, start_pair, (blocked_values, blocked_b, blocked_c, blocked_steps))
    outputs = stacked[0].reshape(row_count, head_count, head_width)
    reach = stacked[1].transpose(1, 0, 2).reshape(head_count, row_count)
    return outputs, final_pair[0], jnp.exp(final_pair[1]), reach


def run_direction(values, b_part, c_part, steps, rate, gain):
    outputs = block_scan(values, b_part, c_part, steps, rate)[0]
    row_count = values.shape[0]
    head_count = steps.shape[0]
    shaped = values.reshape(row_count, head_count, -1)
    return (outputs + gain[None, :, None] * shaped).reshape(row_count, values.shape[1])


def reference(inputs, bc_inputs, dt_raw, conv_inner, conv_state, log_rate, dt_bias, skip_gain):
    length_total = inputs.shape[0]
    width_total = inputs.shape[1]
    head_total = dt_raw.shape[0]
    head_width = width_total // head_total
    group_heads = head_total // 8
    group_width = group_heads * head_width
    state_size = bc_inputs.shape[1] // 2
    bc_float = bc_inputs.astype(jnp.float32)
    forward_bc = conv_silu(bc_float, conv_state)
    reverse_bc = conv_silu(bc_float[::-1], conv_state)
    rate_all = -jnp.exp(log_rate)
    raw_all = dt_raw.astype(jnp.float32)
    comp_raw = jnp.roll(raw_all, head_total // 2, axis=0)
    comp_inputs = jnp.roll(inputs, width_total // 2, axis=1)

    def one_group(group):
        head_start = (group * group_heads).astype(jnp.int32)
        column_start = (group * group_width).astype(jnp.int32)
        weights = lax.dynamic_slice_in_dim(conv_inner, column_start, group_width, 1)
        rate = lax.dynamic_slice_in_dim(rate_all, head_start, group_heads, 0)
        bias = lax.dynamic_slice_in_dim(dt_bias, head_start, group_heads, 0)
        gain = lax.dynamic_slice_in_dim(skip_gain, head_start, group_heads, 0)
        own_values = lax.dynamic_slice_in_dim(inputs, column_start, group_width, 1).astype(jnp.float32)
        fwd_values = conv_silu(own_values, weights)
        fwd_steps = jax.nn.softplus(lax.dynamic_slice_in_dim(raw_all, head_start, group_heads, 0) + bias[:, None])
        forward_y = run_direction(fwd_values, forward_bc[:, :state_size], forward_bc[:, state_size:], fwd_steps, rate, gain)
        mate_values = lax.dynamic_slice_in_dim(comp_inputs, column_start, group_width, 1).astype(jnp.float32)
        rev_values = conv_silu(mate_values[::-1], weights)
        mate_raw = lax.dynamic_slice_in_dim(comp_raw, head_start, group_heads, 0)
        rev_steps = jax.nn.softplus(mate_raw[:, ::-1] + bias[:, None])
        reverse_y = run_direction(rev_values, reverse_bc[:, :state_size], reverse_bc[:, state_size:], rev_steps, rate, gain)[::-1]
        reverse_out = reverse_y.astype(jnp.bfloat16)
        return (forward_y + lax.optimization_barrier(reverse_out).astype(jnp.float32)).astype(jnp.bfloat16)

    pieces = lax.map(one_group, jnp.arange(8, dtype=jnp.int32))
    return pieces.transpose(1, 0, 2).reshape(length_total, width_total)
```

```python
import functools

import jax
import jax.numpy as jnp
from jax import lax
from jax.experimental import pallas as pl
from jax.experimental.pallas import tpu as pltpu
from jax.sharding import PartitionSpec as P

Q = 128
EDGE = 16
HEADS = 4
PIECES = 8
HIGHEST = lax.Precision.HIGHEST
MESH = pl.DeviceIdType.MESH
F32 = jnp.float32
BF16 = jnp.bfloat16


def iota(shape, dim):
    return lax.broadcasted_iota(jnp.int32, shape, dim)


def silu(v):
    h = 0.5 * v
    return h * jnp.tanh(h) + h


def taps(window, weights, begins):
    total = weights[0:1, :] * window[begins[0] : begins[0] + Q]
    for i in range(1, 4):
        total = total + weights[i : i + 1, :] * window[begins[i] : begins[i] + Q]
    return total


def dot(a, b):
    return jnp.dot(a, b, preferred_element_type=F32)


def dot_nt(a, b):
    return lax.dot_general(a, b, (((1,), (1,)), ((), ())), preferred_element_type=F32)


def spread(rows, select):
    high = rows.astype(BF16).astype(F32)
    parts = jnp.concatenate([high, rows - high], axis=0)
    return dot(parts.T.astype(BF16), select)


def kernel(
    seqs, ways,
    x_hbm, bc_hbm, dt_ref, wx_ref, ws_ref, rate_ref, bias_ref, gain_ref,
    out_ref,
    px, pb, pm, gcf, gcr, btr, xsf, xsr, xf, xr, uf, ur, yf, ef, ff, exf, exr,
    run, stot, ra, inc, sin, dmsg, dall,
    local_sem, halo_send, halo_recv, piece_send, piece_recv,
    d_send, d_recv, a_send, a_recv, b_send, b_recv,
):
    rows, width = x_hbm.shape
    chunks = rows // Q
    share = Q // seqs
    here, mine = lax.axis_index("seq"), lax.axis_index("head")
    mate = lax.rem(mine + ways // 2, ways)
    after, before = lax.rem(here + 1, seqs), lax.rem(here + seqs - 1, seqs)

    own_x = pltpu.make_async_copy(x_hbm, px.at[pl.ds(EDGE, rows)], local_sem.at[0])
    own_bc = pltpu.make_async_copy(bc_hbm, pb.at[pl.ds(EDGE, rows)], local_sem.at[1])
    own_x.start()
    own_bc.start()

    barrier = pltpu.get_barrier_semaphore()

    def greet(d, _):
        peer = lax.rem(here + d, seqs)
        pl.semaphore_signal(barrier, inc=1, device_id={"seq": peer, "head": mine}, device_id_type=MESH)
        return 0

    lax.fori_loop(1, seqs, greet, 0)
    for s in (here, after, before):
        pl.semaphore_signal(barrier, inc=1, device_id={"seq": s, "head": mate}, device_id_type=MESH)
    pl.semaphore_wait(barrier, seqs + 2)

    def halo(i, src, dst, s, h):
        return pltpu.make_async_remote_copy(
            src_ref=src, dst_ref=dst, send_sem=halo_send.at[i], recv_sem=halo_recv.at[i],
            device_id={"seq": s, "head": h}, device_id_type=MESH,
        )

    first, last = pl.ds(0, EDGE), pl.ds(rows - EDGE, EDGE)
    low, high = pl.ds(0, EDGE), pl.ds(rows + EDGE, EDGE)
    halos = [
        halo(0, bc_hbm.at[last], pb.at[low], after, mine),
        halo(1, bc_hbm.at[first], pb.at[high], before, mine),
        halo(2, x_hbm.at[last], px.at[low], after, mine),
        halo(3, x_hbm.at[first], pm.at[high], before, mate),
    ]
    for copy in halos:
        copy.start()
    length = rows // PIECES

    def piece(p):
        at = pl.multiple_of(p * length, length)
        return pltpu.make_async_remote_copy(
            src_ref=x_hbm.at[pl.ds(at, length)], dst_ref=pm.at[pl.ds(EDGE + at, length)],
            send_sem=piece_send.at[p], recv_sem=piece_recv.at[p],
            device_id={"seq": here, "head": mate}, device_id_type=MESH,
        )

    def push(i, _):
        piece(PIECES - 1 - i).start()
        return 0

    lax.fori_loop(0, PIECES, push, 0)

    all_heads = dt_ref.shape[0]
    row8, head8 = iota((8, all_heads), 0), iota((8, all_heads), 1)
    owner8 = mine * HEADS + (row8 & (HEADS - 1))
    source8 = owner8 + jnp.where(row8 >= HEADS, all_heads // 2, 0)
    source8 = jnp.where(source8 >= all_heads, source8 - all_heads, source8)
    raw8 = dot((head8 == source8).astype(F32).astype(BF16), dt_ref[...])
    chosen = head8 == owner8

    def pick(values):
        return jnp.sum(jnp.where(chosen, values, 0.0), axis=1, keepdims=True)

    rate8 = pick(-jnp.exp(rate_ref[...]))
    gain8 = pick(gain_ref[...])
    pre = raw8 + pick(bias_ref[...])
    dt8 = jnp.maximum(pre, 0.0) + jnp.log1p(jnp.exp(-jnp.abs(pre)))
    dt = jnp.concatenate([dt8[:, k * Q : (k + 1) * Q] for k in range(chunks)], axis=0)
    logs8 = dt8 * rate8
    logs = jnp.concatenate([logs8[:, k * Q : (k + 1) * Q] for k in range(chunks)], axis=0)
    r, c = iota((Q, Q), 0), iota((Q, Q), 1)
    upto = jnp.dot(logs, (r <= c).astype(F32), precision=HIGHEST, preferred_element_type=F32)
    onward = jnp.dot(logs, (r >= c).astype(F32), precision=HIGHEST, preferred_element_type=F32)
    is_forward = (iota((chunks * 8, Q), 0) & 7) < HEADS
    cum = jnp.where(is_forward, upto, onward)
    half = 0.5 * jnp.sum(logs, axis=1, keepdims=True)
    ef[...] = jnp.exp(cum - half)
    ff[...] = dt * jnp.exp(half - cum)
    per = width // HEADS
    head_row, head_col = iota((chunks * 8, width), 0) & 7, iota((chunks * 8, width), 1) // per
    to_chunk = (iota((chunks, chunks * 8), 1) // 8 == iota((chunks, chunks * 8), 0)).astype(F32)
    totals = []
    for offset, where in ((0, exf), (HEADS, exr)):
        wide = jnp.where(head_row == head_col + offset, half, 0.0)
        summed = jnp.dot(to_chunk, wide, precision=HIGHEST, preferred_element_type=F32)
        where[...] = jnp.exp(summed)
        totals.append(jnp.exp(2.0 * jnp.sum(summed, axis=0, keepdims=True)))
    gain = jnp.sum(
        jnp.where(iota((8, width), 0) == iota((8, width), 1) // per, gain8, 0.0), axis=0, keepdims=True
    )
    sel_row, sel_col = iota((16, width), 0) & 7, iota((16, width), 1) // per
    select_f = (sel_row == sel_col).astype(F32).astype(BF16)
    select_r = (sel_row == sel_col + HEADS).astype(F32).astype(BF16)
    decay = jnp.where(iota((8, width), 0) == 0, totals[0], totals[1])
    dmsg[...] = decay
    dall[here] = decay

    def tell(d):
        return pltpu.make_async_remote_copy(
            src_ref=dmsg, dst_ref=dall.at[here], send_sem=d_send.at[d], recv_sem=d_recv.at[d],
            device_id={"seq": lax.rem(here + d, seqs), "head": mine}, device_id_type=MESH,
        )

    def tell_start(d, _):
        tell(d).start()
        return 0

    lax.fori_loop(1, seqs, tell_start, 0)

    weights_x = wx_ref[:, pl.ds(pl.multiple_of(mine * width, width), width)]
    weights_s = ws_ref[...]

    own_x.wait()
    own_bc.wait()
    for i in range(3):
        halos[i].wait_recv()

    @pl.when(here == 0)
    def _():
        px[pl.ds(0, EDGE), :] = jnp.zeros((EDGE, width), BF16)
        pb[pl.ds(0, EDGE), :] = jnp.zeros((EDGE, width), BF16)

    @pl.when(here == seqs - 1)
    def _():
        pb[pl.ds(rows + EDGE, EDGE), :] = jnp.zeros((EDGE, width), BF16)

    def step_forward(k, state):
        at = pl.multiple_of(k * Q, Q)
        window = pb[pl.ds(at, Q + 2 * EDGE), :].astype(F32)
        fwd = silu(taps(window, weights_s, [EDGE - 3, EDGE - 2, EDGE - 1, EDGE]))
        rev = silu(taps(window, weights_s, [EDGE + 3, EDGE + 2, EDGE + 1, EDGE]))
        bf, cf = fwd[:, :Q].astype(BF16), fwd[:, Q:].astype(BF16)
        br, cr = rev[:, :Q].astype(BF16), rev[:, Q:].astype(BF16)
        gcf[pl.ds(at, Q), Q:] = cf
        gcr[pl.ds(at, Q), Q:] = cr
        gcf[pl.ds(at, Q), :Q] = jnp.where(r >= c, dot_nt(cf, bf), 0.0).astype(BF16)
        gcr[pl.ds(at, Q), :Q] = jnp.where(r <= c, dot_nt(cr, br), 0.0).astype(BF16)
        btr[pl.ds(at, Q), :] = rev[:, :Q].T.astype(BF16)
        window = px[pl.ds(at, Q + EDGE), :].astype(F32)
        value = silu(taps(window, weights_x, [EDGE - 3, EDGE - 2, EDGE - 1, EDGE]))
        xf[pl.ds(at, Q), :] = value
        scaled = (value * spread(ff[pl.ds(pl.multiple_of(k * 8, 8), 8), :], select_f)).astype(BF16)
        xsf[k, :Q, :] = scaled
        update = dot(fwd[:, :Q].T.astype(BF16), scaled)
        uf[k] = update
        e = exf[pl.ds(k, 1), :]
        return e * (e * state + update)

    stot[0] = lax.fori_loop(0, chunks, step_forward, jnp.zeros((Q, width), F32))

    def to_owner(way, d):
        peer = lax.rem(here + d, seqs)
        return pltpu.make_async_remote_copy(
            src_ref=stot.at[way, pl.ds(pl.multiple_of(peer * share, share), share)],
            dst_ref=ra.at[way, here], send_sem=a_send.at[way, d], recv_sem=a_recv.at[way, d],
            device_id={"seq": peer, "head": mine}, device_id_type=MESH,
        )

    def from_owner(way, d):
        peer = lax.rem(here + d, seqs)
        return pltpu.make_async_remote_copy(
            src_ref=inc.at[way, peer],
            dst_ref=sin.at[way, pl.ds(pl.multiple_of(here * share, share), share)],
            send_sem=b_send.at[way, d], recv_sem=b_recv.at[way, d],
            device_id={"seq": peer, "head": mine}, device_id_type=MESH,
        )

    mine_rows = pl.ds(pl.multiple_of(here * share, share), share)

    def states_out(way):
        def go(d, _):
            to_owner(way, d).start()
            return 0

        lax.fori_loop(1, seqs, go, 0)
        ra[way, here] = stot[way, mine_rows, :]

    def states_back(way):
        def arrive(d, _):
            to_owner(way, d).wait_recv()
            return 0

        lax.fori_loop(1, seqs, arrive, 0)

        def hop(i, entering):
            at = i if way == 0 else seqs - 1 - i
            inc[way, at] = entering
            return dall[at, way : way + 1, :] * entering + ra[way, at]

        lax.fori_loop(0, seqs, hop, jnp.zeros((share, width), F32))

        def go(d, _):
            from_owner(way, d).start()
            return 0

        lax.fori_loop(1, seqs, go, 0)
        sin[way, mine_rows, :] = inc[way, here]

    def states_in(way):
        def arrive(d, _):
            from_owner(way, d).wait_recv()
            return 0

        lax.fori_loop(1, seqs, arrive, 0)

    def step_reverse(k):
        at = pl.multiple_of(k * Q, Q)
        window = pm[pl.ds(EDGE + at, Q + EDGE), :].astype(F32)
        value = silu(taps(window, weights_x, [3, 2, 1, 0]))
        xr[pl.ds(at, Q), :] = value
        scaled = (value * spread(ff[pl.ds(pl.multiple_of(k * 8, 8), 8), :], select_r)).astype(BF16)
        xsr[k, :Q, :] = scaled
        update = dot(btr[pl.ds(at, Q), :], scaled)
        ur[k] = update
        e = exr[pl.ds(k, 1), :]
        run[...] = e * (e * run[...] + update)

    each = chunks // PIECES

    def pieces(start, stop):
        def one(i, _):
            p = PIECES - 1 - i
            piece(p).wait_recv()

            def inner(j, _):
                step_reverse(p * each + each - 1 - j)
                return 0

            lax.fori_loop(0, each, inner, 0)
            return 0

        lax.fori_loop(start, stop, one, 0)

    states_out(0)
    run[...] = jnp.zeros((Q, width), F32)
    halos[3].wait_recv()

    @pl.when(here == seqs - 1)
    def _():
        pm[pl.ds(rows + EDGE, EDGE), :] = jnp.zeros((EDGE, width), BF16)

    pieces(0, 2)

    def told(d, _):
        tell(d).wait_recv()
        return 0

    lax.fori_loop(1, seqs, told, 0)
    states_back(0)
    pieces(2, 4)
    states_in(0)

    def finish_forward(k, state):
        at = pl.multiple_of(k * Q, Q)
        e = exf[pl.ds(k, 1), :]
        entering = e * state
        xsf[k, Q:, :] = entering.astype(BF16)
        y = dot(gcf[pl.ds(at, Q), :], xsf[k])
        scale = spread(ef[pl.ds(pl.multiple_of(k * 8, 8), 8), :], select_f)
        yf[pl.ds(at, Q), :] = scale * y + gain * xf[pl.ds(at, Q), :]
        return e * (entering + uf[k])

    lax.fori_loop(0, chunks, finish_forward, sin[0])
    pieces(4, PIECES)
    stot[1] = run[...]
    states_out(1)
    states_back(1)
    states_in(1)

    def finish_reverse(i, state):
        k = chunks - 1 - i
        at = pl.multiple_of(k * Q, Q)
        e = exr[pl.ds(k, 1), :]
        entering = e * state
        xsr[k, Q:, :] = entering.astype(BF16)
        y = dot(gcr[pl.ds(at, Q), :], xsr[k])
        scale = spread(ef[pl.ds(pl.multiple_of(k * 8, 8), 8), :], select_r)
        back = (scale * y + gain * xr[pl.ds(at, Q), :]).astype(BF16)
        out_ref[pl.ds(at, Q), :] = (yf[pl.ds(at, Q), :] + back.astype(F32)).astype(BF16)
        return e * (entering + ur[k])

    lax.fori_loop(0, chunks, finish_reverse, sin[1])

    for copy in halos:
        copy.wait_send()

    def sent_piece(p, _):
        piece(p).wait_send()
        return 0

    lax.fori_loop(0, PIECES, sent_piece, 0)

    def sent(d, _):
        tell(d).wait_send()
        for way in (0, 1):
            to_owner(way, d).wait_send()
            from_owner(way, d).wait_send()
        return 0

    lax.fori_loop(1, seqs, sent, 0)


def per_device(inputs, bc_inputs, dt_raw, conv_inner, conv_state, log_rate, dt_bias, skip_gain):
    seqs, ways = lax.axis_size("seq"), lax.axis_size("head")
    rows, width = inputs.shape
    chunks, share = rows // Q, Q // seqs
    anywhere = pl.BlockSpec(memory_space=pl.ANY)
    vmem = pl.BlockSpec(memory_space=pltpu.VMEM)
    padded = pltpu.VMEM((rows + 2 * EDGE, width), BF16)
    dma = pltpu.SemaphoreType.DMA
    return pl.pallas_call(
        functools.partial(kernel, seqs, ways),
        out_shape=jax.ShapeDtypeStruct((rows, width), BF16),
        in_specs=[anywhere, anywhere] + [vmem] * 6,
        out_specs=vmem,
        scratch_shapes=[
            padded, padded, padded,
            pltpu.VMEM((rows, 2 * Q), BF16), pltpu.VMEM((rows, 2 * Q), BF16), pltpu.VMEM((rows, Q), BF16),
            pltpu.VMEM((chunks, 2 * Q, width), BF16), pltpu.VMEM((chunks, 2 * Q, width), BF16),
            pltpu.VMEM((rows, width), F32), pltpu.VMEM((rows, width), F32),
            pltpu.VMEM((chunks, Q, width), F32), pltpu.VMEM((chunks, Q, width), F32),
            pltpu.VMEM((rows, width), F32),
            pltpu.VMEM((chunks * 8, Q), F32), pltpu.VMEM((chunks * 8, Q), F32),
            pltpu.VMEM((chunks, width), F32), pltpu.VMEM((chunks, width), F32),
            pltpu.VMEM((Q, width), F32), pltpu.VMEM((2, Q, width), F32),
            pltpu.VMEM((2, seqs, share, width), F32), pltpu.VMEM((2, seqs, share, width), F32),
            pltpu.VMEM((2, Q, width), F32),
            pltpu.VMEM((8, width), F32), pltpu.VMEM((seqs, 8, width), F32),
            dma((2,)), dma((4,)), dma((4,)), dma((PIECES,)), dma((PIECES,)),
            dma((seqs,)), dma((seqs,)), dma((2, seqs)), dma((2, seqs)), dma((2, seqs)), dma((2, seqs)),
        ],
        compiler_params=pltpu.CompilerParams(
            collective_id=0, has_side_effects=True, vmem_limit_bytes=48 * 2**20
        ),
    )(
        inputs, bc_inputs, dt_raw, conv_inner, conv_state,
        log_rate[None, :], dt_bias[None, :], skip_gain[None, :],
    )


def solution(mesh):
    return jax.shard_map(
        per_device,
        mesh=mesh,
        in_specs=(P("seq", "head"), P("seq", None), P(None, "seq"), P(), P(), P(), P(), P()),
        out_specs=P("seq", "head"),
        check_vma=False,
    )
```

```python
import functools

import jax
import jax.numpy as jnp
from jax import lax
from jax.experimental import pallas as pl
from jax.experimental.pallas import tpu as pltpu
from jax.sharding import PartitionSpec as P

Q = 128
EDGE = 16
HEADS = 4
PIECES = 8
HIGHEST = lax.Precision.HIGHEST
MESH = pl.DeviceIdType.MESH
F32 = jnp.float32
BF16 = jnp.bfloat16


def iota(shape, dim):
    return lax.broadcasted_iota(jnp.int32, shape, dim)


def silu(v):
    h = 0.5 * v
    return h * jnp.tanh(h) + h


def taps(window, weights, begins):
    total = weights[0:1, :] * window[begins[0] : begins[0] + Q]
    for i in range(1, 4):
        total = total + weights[i : i + 1, :] * window[begins[i] : begins[i] + Q]
    return total


def dot(a, b):
    return jnp.dot(a, b, preferred_element_type=F32)


def dot_nt(a, b):
    return lax.dot_general(a, b, (((1,), (1,)), ((), ())), preferred_element_type=F32)


def spread(rows, select):
    high = rows.astype(BF16).astype(F32)
    parts = jnp.concatenate([high, rows - high], axis=0)
    return dot(parts.T.astype(BF16), select)


def kernel(
    seqs, ways,
    x_hbm, bc_hbm, dt_hbm, wx_hbm, ws_ref, rate_ref, bias_ref, gain_ref,
    out_ref,
    dt_ref, wx_ref, px, pb, pm, gcf, gcr, btr, xsf, xsr, xf, xr, uf, ur, yf, ef, ff, exf, exr,
    run, stot, ra, inc, sin, dmsg, dall,
    local_sem, halo_send, halo_recv, piece_send, piece_recv,
    d_send, d_recv, a_send, a_recv, b_send, b_recv,
):
    rows, width = x_hbm.shape
    chunks = rows // Q
    share = Q // seqs
    here, mine = lax.axis_index("seq"), lax.axis_index("head")
    mate = (mine + ways // 2) & (ways - 1)
    after, before = (here + 1) & (seqs - 1), (here - 1) & (seqs - 1)

    own_x = pltpu.make_async_copy(x_hbm, px.at[pl.ds(EDGE, rows)], local_sem.at[0])
    own_bc = pltpu.make_async_copy(bc_hbm, pb.at[pl.ds(EDGE, rows)], local_sem.at[1])
    own_dt = pltpu.make_async_copy(dt_hbm, dt_ref, local_sem.at[2])
    columns = pl.ds(pl.multiple_of(mine * width, width), width)
    own_w = pltpu.make_async_copy(wx_hbm.at[:, columns], wx_ref, local_sem.at[3])

    barrier = pltpu.get_barrier_semaphore()

    def greet(d, _):
        peer = (here + d) & (seqs - 1)
        pl.semaphore_signal(barrier, inc=1, device_id={"seq": peer, "head": mine}, device_id_type=MESH)
        return 0

    lax.fori_loop(1, seqs, greet, 0)
    for s in (here, after, before):
        pl.semaphore_signal(barrier, inc=1, device_id={"seq": s, "head": mate}, device_id_type=MESH)
    own_dt.start()
    own_bc.start()
    own_x.start()
    own_w.start()
    own_dt.wait()

    all_heads = dt_ref.shape[0]
    row8, head8 = iota((8, all_heads), 0), iota((8, all_heads), 1)
    owner8 = mine * HEADS + (row8 & (HEADS - 1))
    source8 = owner8 + jnp.where(row8 >= HEADS, all_heads // 2, 0)
    source8 = jnp.where(source8 >= all_heads, source8 - all_heads, source8)
    raw8 = dot((head8 == source8).astype(F32).astype(BF16), dt_ref[...])
    chosen = head8 == owner8

    def pick(values):
        return jnp.sum(jnp.where(chosen, values, 0.0), axis=1, keepdims=True)

    rate8 = pick(-jnp.exp(rate_ref[...]))
    gain8 = pick(gain_ref[...])
    pre = raw8 + pick(bias_ref[...])
    dt8 = jnp.maximum(pre, 0.0) + jnp.log1p(jnp.exp(-jnp.abs(pre)))
    dt = jnp.concatenate([dt8[:, k * Q : (k + 1) * Q] for k in range(chunks)], axis=0)
    logs8 = dt8 * rate8
    logs = jnp.concatenate([logs8[:, k * Q : (k + 1) * Q] for k in range(chunks)], axis=0)
    r, c = iota((Q, Q), 0), iota((Q, Q), 1)
    upto = jnp.dot(logs, (r <= c).astype(F32), precision=HIGHEST, preferred_element_type=F32)
    onward = jnp.dot(logs, (r >= c).astype(F32), precision=HIGHEST, preferred_element_type=F32)
    is_forward = (iota((chunks * 8, Q), 0) & 7) < HEADS
    cum = jnp.where(is_forward, upto, onward)
    half = 0.5 * jnp.sum(logs, axis=1, keepdims=True)
    ef[...] = jnp.exp(cum - half)
    ff[...] = dt * jnp.exp(half - cum)
    per = width // HEADS
    head_row, head_col = iota((chunks * 8, width), 0) & 7, iota((chunks * 8, width), 1) // per
    to_chunk = (iota((chunks, chunks * 8), 1) // 8 == iota((chunks, chunks * 8), 0)).astype(F32)
    for offset, where in ((0, exf), (HEADS, exr)):
        wide = jnp.where(head_row == head_col + offset, half, 0.0)
        summed = jnp.dot(to_chunk, wide, precision=HIGHEST, preferred_element_type=F32)
        where[...] = jnp.exp(summed)
    gain = jnp.sum(
        jnp.where(iota((8, width), 0) == iota((8, width), 1) // per, gain8, 0.0), axis=0, keepdims=True
    )
    sel_row, sel_col = iota((16, width), 0) & 7, iota((16, width), 1) // per
    select_f = (sel_row == sel_col).astype(F32).astype(BF16)
    select_r = (sel_row == sel_col + HEADS).astype(F32).astype(BF16)
    all_logs = sum(half[8 * k : 8 * k + 8, :] for k in range(chunks))
    decay = jnp.broadcast_to(jnp.exp(2.0 * all_logs), (8, Q))
    pl.semaphore_wait(barrier, seqs + 2)

    def halo(i, src, dst, s, h):
        return pltpu.make_async_remote_copy(
            src_ref=src, dst_ref=dst, send_sem=halo_send.at[i], recv_sem=halo_recv.at[i],
            device_id={"seq": s, "head": h}, device_id_type=MESH,
        )

    first, last = pl.ds(0, EDGE), pl.ds(rows - EDGE, EDGE)
    low, high = pl.ds(0, EDGE), pl.ds(rows + EDGE, EDGE)
    halos = [
        halo(0, bc_hbm.at[last], pb.at[low], after, mine),
        halo(1, bc_hbm.at[first], pb.at[high], before, mine),
        halo(2, x_hbm.at[last], px.at[low], after, mine),
        halo(3, x_hbm.at[first], pm.at[high], before, mate),
    ]
    for copy in halos:
        copy.start()
    length = rows // PIECES

    def piece(p):
        at = pl.multiple_of(p * length, length)
        return pltpu.make_async_remote_copy(
            src_ref=x_hbm.at[pl.ds(at, length)], dst_ref=pm.at[pl.ds(EDGE + at, length)],
            send_sem=piece_send.at[p], recv_sem=piece_recv.at[p],
            device_id={"seq": here, "head": mate}, device_id_type=MESH,
        )

    def push(i, _):
        piece(PIECES - 1 - i).start()
        return 0

    lax.fori_loop(0, PIECES, push, 0)

    dmsg[...] = decay
    dall[here] = decay

    def tell(d):
        return pltpu.make_async_remote_copy(
            src_ref=dmsg, dst_ref=dall.at[here], send_sem=d_send, recv_sem=d_recv,
            device_id={"seq": (here + d) & (seqs - 1), "head": mine}, device_id_type=MESH,
        )

    def tell_start(d, _):
        tell(d).start()
        return 0

    lax.fori_loop(1, seqs, tell_start, 0)

    own_w.wait()
    weights_x = wx_ref[...]
    weights_s = ws_ref[...]

    own_x.wait()
    own_bc.wait()
    for i in range(3):
        halos[i].wait_recv()

    @pl.when(here == 0)
    def _():
        px[pl.ds(0, EDGE), :] = jnp.zeros((EDGE, width), BF16)
        pb[pl.ds(0, EDGE), :] = jnp.zeros((EDGE, width), BF16)

    @pl.when(here == seqs - 1)
    def _():
        pb[pl.ds(rows + EDGE, EDGE), :] = jnp.zeros((EDGE, width), BF16)

    def step_forward(k, state):
        at = pl.multiple_of(k * Q, Q)
        window = pb[pl.ds(at, Q + 2 * EDGE), :].astype(F32)
        fwd = silu(taps(window, weights_s, [EDGE - 3, EDGE - 2, EDGE - 1, EDGE]))
        rev = silu(taps(window, weights_s, [EDGE + 3, EDGE + 2, EDGE + 1, EDGE]))
        bf, cf = fwd[:, :Q].astype(BF16), fwd[:, Q:].astype(BF16)
        br, cr = rev[:, :Q].astype(BF16), rev[:, Q:].astype(BF16)
        gcf[pl.ds(at, Q), Q:] = cf
        gcr[pl.ds(at, Q), Q:] = cr
        gcf[pl.ds(at, Q), :Q] = jnp.where(r >= c, dot_nt(cf, bf), 0.0).astype(BF16)
        gcr[pl.ds(at, Q), :Q] = jnp.where(r <= c, dot_nt(cr, br), 0.0).astype(BF16)
        btr[pl.ds(at, Q), :] = rev[:, :Q].T.astype(BF16)
        window = px[pl.ds(at, Q + EDGE), :].astype(F32)
        value = silu(taps(window, weights_x, [EDGE - 3, EDGE - 2, EDGE - 1, EDGE]))
        xf[pl.ds(at, Q), :] = value
        scaled = (value * spread(ff[pl.ds(pl.multiple_of(k * 8, 8), 8), :], select_f)).astype(BF16)
        xsf[k, :Q, :] = scaled
        update = dot(fwd[:, :Q].T.astype(BF16), scaled)
        uf[k] = update
        e = exf[pl.ds(k, 1), :]
        return e * (e * state + update)

    stot[0] = lax.fori_loop(0, chunks, step_forward, jnp.zeros((Q, width), F32))

    def to_owner(way, d):
        peer = (here + d) & (seqs - 1)
        return pltpu.make_async_remote_copy(
            src_ref=stot.at[way, pl.ds(pl.multiple_of(peer * share, share), share)],
            dst_ref=ra.at[way, here], send_sem=a_send.at[way], recv_sem=a_recv.at[way],
            device_id={"seq": peer, "head": mine}, device_id_type=MESH,
        )

    def from_owner(way, d):
        peer = (here + d) & (seqs - 1)
        return pltpu.make_async_remote_copy(
            src_ref=inc.at[way, peer],
            dst_ref=sin.at[way, pl.ds(pl.multiple_of(here * share, share), share)],
            send_sem=b_send.at[way], recv_sem=b_recv.at[way],
            device_id={"seq": peer, "head": mine}, device_id_type=MESH,
        )

    mine_rows = pl.ds(pl.multiple_of(here * share, share), share)

    def others(buffer, way, sem):
        span = buffer.at[way, pl.ds(0, seqs - 1)]
        pltpu.make_async_copy(span, span, sem.at[way]).wait()

    def states_out(way):
        def go(d, _):
            to_owner(way, d).start()
            return 0

        lax.fori_loop(1, seqs, go, 0)
        ra[way, here] = stot[way, mine_rows, :]

    def states_back(way):
        others(ra, way, a_recv)
        left = iota((1, Q), 1) < Q // 2

        def hop(i, entering):
            at = i if way == 0 else seqs - 1 - i
            inc[way, at] = entering
            d = [dall[at, HEADS * way + h : HEADS * way + h + 1, :] for h in range(HEADS)]
            decay = jnp.concatenate([jnp.where(left, d[0], d[1]), jnp.where(left, d[2], d[3])], axis=1)
            return decay * entering + ra[way, at]

        lax.fori_loop(0, seqs, hop, jnp.zeros((share, width), F32))

        def go(d, _):
            from_owner(way, d).start()
            return 0

        lax.fori_loop(1, seqs, go, 0)
        sin[way, mine_rows, :] = inc[way, here]

    def states_in(way):
        others(inc, way, b_recv)

    def step_reverse(k):
        at = pl.multiple_of(k * Q, Q)
        window = pm[pl.ds(EDGE + at, Q + EDGE), :].astype(F32)
        value = silu(taps(window, weights_x, [3, 2, 1, 0]))
        xr[pl.ds(at, Q), :] = value
        scaled = (value * spread(ff[pl.ds(pl.multiple_of(k * 8, 8), 8), :], select_r)).astype(BF16)
        xsr[k, :Q, :] = scaled
        update = dot(btr[pl.ds(at, Q), :], scaled)
        ur[k] = update
        e = exr[pl.ds(k, 1), :]
        run[...] = e * (e * run[...] + update)

    each = chunks // PIECES

    def pieces(start, stop):
        def one(i, _):
            p = PIECES - 1 - i
            piece(p).wait_recv()

            def inner(j, _):
                step_reverse(p * each + each - 1 - j)
                return 0

            lax.fori_loop(0, each, inner, 0)
            return 0

        lax.fori_loop(start, stop, one, 0)

    states_out(0)
    run[...] = jnp.zeros((Q, width), F32)
    halos[3].wait_recv()

    @pl.when(here == seqs - 1)
    def _():
        pm[pl.ds(rows + EDGE, EDGE), :] = jnp.zeros((EDGE, width), BF16)

    pieces(0, PIECES // 2)

    everyone = dall.at[pl.ds(0, seqs - 1)]
    pltpu.make_async_copy(everyone, everyone, d_recv).wait()
    states_back(0)
    pieces(PIECES // 2, PIECES)
    stot[1] = run[...]
    states_out(1)
    states_in(0)

    def finish_forward(k, state):
        at = pl.multiple_of(k * Q, Q)
        e = exf[pl.ds(k, 1), :]
        entering = e * state
        xsf[k, Q:, :] = entering.astype(BF16)
        y = dot(gcf[pl.ds(at, Q), :], xsf[k])
        scale = spread(ef[pl.ds(pl.multiple_of(k * 8, 8), 8), :], select_f)
        yf[pl.ds(at, Q), :] = scale * y + gain * xf[pl.ds(at, Q), :]
        return e * (entering + uf[k])

    lax.fori_loop(0, chunks // 2, lambda i, st: finish_forward(2 * i + 1, finish_forward(2 * i, st)), sin[0])
    states_back(1)
    states_in(1)

    def finish_reverse(i, state):
        k = chunks - 1 - i
        at = pl.multiple_of(k * Q, Q)
        e = exr[pl.ds(k, 1), :]
        entering = e * state
        xsr[k, Q:, :] = entering.astype(BF16)
        y = dot(gcr[pl.ds(at, Q), :], xsr[k])
        scale = spread(ef[pl.ds(pl.multiple_of(k * 8, 8), 8), :], select_r)
        back = (scale * y + gain * xr[pl.ds(at, Q), :]).astype(BF16)
        out_ref[pl.ds(at, Q), :] = (yf[pl.ds(at, Q), :] + back.astype(F32)).astype(BF16)
        return e * (entering + ur[k])

    lax.fori_loop(0, chunks // 2, lambda i, st: finish_reverse(2 * i + 1, finish_reverse(2 * i, st)), sin[1])

    for copy in halos:
        copy.wait_send()

    for p in range(PIECES):
        piece(p).wait_send()

    pltpu.make_async_copy(everyone, everyone, d_send).wait()
    for way in (0, 1):
        others(ra, way, a_send)
        others(inc, way, b_send)


def per_device(inputs, bc_inputs, dt_raw, conv_inner, conv_state, log_rate, dt_bias, skip_gain):
    seqs, ways = lax.axis_size("seq"), lax.axis_size("head")
    rows, width = inputs.shape
    chunks, share = rows // Q, Q // seqs
    anywhere = pl.BlockSpec(memory_space=pl.ANY)
    vmem = pl.BlockSpec(memory_space=pltpu.VMEM)
    padded = pltpu.VMEM((rows + 2 * EDGE, width), BF16)
    dma = pltpu.SemaphoreType.DMA
    return pl.pallas_call(
        functools.partial(kernel, seqs, ways),
        out_shape=jax.ShapeDtypeStruct((rows, width), BF16),
        in_specs=[anywhere] * 4 + [vmem] * 4,
        out_specs=vmem,
        scratch_shapes=[
            pltpu.VMEM(dt_raw.shape, BF16), pltpu.VMEM((4, width), F32), padded, padded, padded,
            pltpu.VMEM((rows, 2 * Q), BF16), pltpu.VMEM((rows, 2 * Q), BF16), pltpu.VMEM((rows, Q), BF16),
            pltpu.VMEM((chunks, 2 * Q, width), BF16), pltpu.VMEM((chunks, 2 * Q, width), BF16),
            pltpu.VMEM((rows, width), F32), pltpu.VMEM((rows, width), F32),
            pltpu.VMEM((chunks, Q, width), F32), pltpu.VMEM((chunks, Q, width), F32),
            pltpu.VMEM((rows, width), F32),
            pltpu.VMEM((chunks * 8, Q), F32), pltpu.VMEM((chunks * 8, Q), F32),
            pltpu.VMEM((chunks, width), F32), pltpu.VMEM((chunks, width), F32),
            pltpu.VMEM((Q, width), F32), pltpu.VMEM((2, Q, width), F32),
            pltpu.VMEM((2, seqs, share, width), F32), pltpu.VMEM((2, seqs, share, width), F32),
            pltpu.VMEM((2, Q, width), F32),
            pltpu.VMEM((8, Q), F32), pltpu.VMEM((seqs, 8, Q), F32),
            dma((4,)), dma((4,)), dma((4,)), dma((PIECES,)), dma((PIECES,)),
            dma, dma, dma((2,)), dma((2,)), dma((2,)), dma((2,)),
        ],
        compiler_params=pltpu.CompilerParams(
            collective_id=0, has_side_effects=True, vmem_limit_bytes=60 * 2**20
        ),
    )(
        inputs, bc_inputs, dt_raw, conv_inner, conv_state,
        log_rate[None, :], dt_bias[None, :], skip_gain[None, :],
    )


def solution(mesh):
    return jax.shard_map(
        per_device,
        mesh=mesh,
        in_specs=(P("seq", "head"), P("seq", None), P(None, "seq"), P(), P(), P(), P(), P()),
        out_specs=P("seq", "head"),
        check_vma=False,
    )
```

```python
import functools

import jax
import jax.numpy as jnp
from jax import lax
from jax.experimental import pallas as pl
from jax.experimental.pallas import tpu as pltpu
from jax.sharding import PartitionSpec as P

Q = 128
EDGE = 16
HEADS = 4
PIECES = 4
HIGHEST = lax.Precision.HIGHEST
MESH = pl.DeviceIdType.MESH
F32 = jnp.float32
BF16 = jnp.bfloat16


def iota(shape, dim):
    return lax.broadcasted_iota(jnp.int32, shape, dim)


def silu(v):
    h = 0.5 * v
    return h * jnp.tanh(h) + h


def taps(window, weights, begins):
    total = weights[0:1, :] * window[begins[0] : begins[0] + Q]
    for i in range(1, 4):
        total = total + weights[i : i + 1, :] * window[begins[i] : begins[i] + Q]
    return total


def dot(a, b):
    return jnp.dot(a, b, preferred_element_type=F32)


def dot_nt(a, b):
    return lax.dot_general(a, b, (((1,), (1,)), ((), ())), preferred_element_type=F32)


def spread(rows, select):
    high = rows.astype(BF16).astype(F32)
    parts = jnp.concatenate([high, rows - high], axis=0)
    return dot(parts.T.astype(BF16), select)


def kernel(
    seqs, ways,
    x_hbm, bc_hbm, dt_hbm, wx_hbm, ws_ref, rate_ref, bias_ref, gain_ref,
    out_ref,
    dt_ref, wx_ref, wm_ref, px, pb, pm, gcf, gcr, btr, xsf, xsr, xf, xr, uf, ur, yf, ef, ff, exf, exr,
    away, back_in, tot_f, tot_r, got_f, got_r, inc_f, inc_r, in_f, in_r, dmsg, dall,
    local_sem, halo_send, halo_recv, piece_send, piece_recv,
    out_send, out_recv, d_send, d_recv, a_send, a_recv, b_send, b_recv,
):
    rows, width = x_hbm.shape
    chunks = rows // Q
    share = Q // seqs
    wing = width // 2
    here, mine = lax.axis_index("seq"), lax.axis_index("head")
    mate = (mine + ways // 2) & (ways - 1)
    after, before = (here + 1) & (seqs - 1), (here - 1) & (seqs - 1)

    own_x = pltpu.make_async_copy(x_hbm, px.at[pl.ds(EDGE, rows)], local_sem.at[0])
    own_bc = pltpu.make_async_copy(bc_hbm, pb.at[pl.ds(EDGE, rows)], local_sem.at[1])
    own_dt = pltpu.make_async_copy(dt_hbm, dt_ref, local_sem.at[2])
    columns = pl.ds(pl.multiple_of(mine * width, width), width)
    theirs = pl.ds(pl.multiple_of(mate * width + wing, wing), wing)
    mate_w = pltpu.make_async_copy(wx_hbm.at[:, theirs], wm_ref, local_sem.at[4])
    own_w = pltpu.make_async_copy(wx_hbm.at[:, columns], wx_ref, local_sem.at[3])

    barrier = pltpu.get_barrier_semaphore()

    def greet(d, _):
        peer = (here + d) & (seqs - 1)
        pl.semaphore_signal(barrier, inc=1, device_id={"seq": peer, "head": mine}, device_id_type=MESH)
        return 0

    lax.fori_loop(1, seqs, greet, 0)
    for s in (here, after, before):
        pl.semaphore_signal(barrier, inc=1, device_id={"seq": s, "head": mate}, device_id_type=MESH)
    own_dt.start()
    own_bc.start()
    own_x.start()
    own_w.start()
    mate_w.start()
    own_dt.wait()

    all_heads = dt_ref.shape[0]
    row8, head8 = iota((8, all_heads), 0), iota((8, all_heads), 1)
    owner8 = jnp.where(row8 < 6, mine, mate) * HEADS + (row8 & (HEADS - 1))
    source8 = jnp.where((row8 == 4) | (row8 == 5), mate, mine) * HEADS + (row8 & (HEADS - 1))
    raw8 = dot((head8 == source8).astype(F32).astype(BF16), dt_ref[...])
    chosen = head8 == owner8

    def pick(values):
        return jnp.sum(jnp.where(chosen, values, 0.0), axis=1, keepdims=True)

    rate8 = pick(-jnp.exp(rate_ref[...]))
    gain8 = pick(gain_ref[...])
    pre = raw8 + pick(bias_ref[...])
    dt8 = jnp.maximum(pre, 0.0) + jnp.log1p(jnp.exp(-jnp.abs(pre)))
    dt = jnp.concatenate([dt8[:, k * Q : (k + 1) * Q] for k in range(chunks)], axis=0)
    logs8 = dt8 * rate8
    logs = jnp.concatenate([logs8[:, k * Q : (k + 1) * Q] for k in range(chunks)], axis=0)
    r, c = iota((Q, Q), 0), iota((Q, Q), 1)
    upto = jnp.dot(logs, (r <= c).astype(F32), precision=HIGHEST, preferred_element_type=F32)
    onward = jnp.dot(logs, (r >= c).astype(F32), precision=HIGHEST, preferred_element_type=F32)
    is_forward = (iota((chunks * 8, Q), 0) & 7) < HEADS
    cum = jnp.where(is_forward, upto, onward)
    half = 0.5 * jnp.sum(logs, axis=1, keepdims=True)
    ef[...] = jnp.exp(cum - half)
    ff[...] = dt * jnp.exp(half - cum)
    per = width // HEADS
    head_row, head_col = iota((chunks * 8, width), 0) & 7, iota((chunks * 8, width), 1) // per
    to_chunk = (iota((chunks, chunks * 8), 1) // 8 == iota((chunks, chunks * 8), 0)).astype(F32)
    for offset, where in ((0, exf), (HEADS, exr)):
        wide = jnp.where(head_row == head_col + offset, half, 0.0)
        summed = jnp.dot(to_chunk, wide, precision=HIGHEST, preferred_element_type=F32)
        where[...] = jnp.exp(summed)
    gain_row, gain_col = iota((8, width), 0), iota((8, width), 1) // per
    gain_f = jnp.sum(jnp.where(gain_row == gain_col, gain8, 0.0), axis=0, keepdims=True)
    gain_r = jnp.sum(jnp.where(gain_row == gain_col + HEADS, gain8, 0.0), axis=0, keepdims=True)
    sel_row, sel_col = iota((16, width), 0) & 7, iota((16, width), 1) // per
    select_f = (sel_row == sel_col).astype(F32).astype(BF16)
    select_r = (sel_row == sel_col + HEADS).astype(F32).astype(BF16)
    all_logs = sum(half[8 * k : 8 * k + 8, :] for k in range(chunks))
    decay = jnp.broadcast_to(jnp.exp(2.0 * all_logs), (8, Q))
    pl.semaphore_wait(barrier, seqs + 2)

    def halo(i, src, dst, s, h):
        return pltpu.make_async_remote_copy(
            src_ref=src, dst_ref=dst, send_sem=halo_send.at[i], recv_sem=halo_recv.at[i],
            device_id={"seq": s, "head": h}, device_id_type=MESH,
        )

    first, last = pl.ds(0, EDGE), pl.ds(rows - EDGE, EDGE)
    low, high = pl.ds(0, EDGE), pl.ds(rows + EDGE, EDGE)
    halos = [
        halo(0, bc_hbm.at[last], pb.at[low], after, mine),
        halo(1, bc_hbm.at[first], pb.at[high], before, mine),
        halo(2, x_hbm.at[last], px.at[low], after, mine),
        halo(3, x_hbm.at[first], px.at[high], before, mine),
        halo(4, x_hbm.at[first, pl.ds(0, wing)], pm.at[high], before, mate),
    ]
    for copy in halos:
        copy.start()
    length = rows // PIECES

    def piece(p):
        at = pl.multiple_of(p * length, length)
        return pltpu.make_async_remote_copy(
            src_ref=x_hbm.at[pl.ds(at, length), pl.ds(0, wing)], dst_ref=pm.at[pl.ds(EDGE + at, length)],
            send_sem=piece_send.at[p], recv_sem=piece_recv.at[p],
            device_id={"seq": here, "head": mate}, device_id_type=MESH,
        )

    def push(i, _):
        piece(PIECES - 1 - i).start()
        return 0

    lax.fori_loop(0, PIECES, push, 0)

    dmsg[...] = decay
    dall[here] = decay

    def tell(d):
        return pltpu.make_async_remote_copy(
            src_ref=dmsg, dst_ref=dall.at[here], send_sem=d_send, recv_sem=d_recv,
            device_id={"seq": (here + d) & (seqs - 1), "head": mine}, device_id_type=MESH,
        )

    def tell_start(d, _):
        tell(d).start()
        return 0

    lax.fori_loop(1, seqs, tell_start, 0)

    own_w.wait()
    mate_w.wait()
    weights_x = wx_ref[...]
    weights_r = (weights_x[:, :wing], wm_ref[...])
    weights_s = ws_ref[...]

    own_x.wait()
    own_bc.wait()
    def by(n, body):
        def several(i, state):
            for j in range(n):
                state = body(n * i + j, state)
            return state

        return several

    def arrive_halos():
        for i in range(4):
            halos[i].wait_recv()

        @pl.when(here == 0)
        def _():
            px[pl.ds(0, EDGE), :] = jnp.zeros((EDGE, width), BF16)
            pb[pl.ds(0, EDGE), :] = jnp.zeros((EDGE, width), BF16)

        @pl.when(here == seqs - 1)
        def _():
            pb[pl.ds(rows + EDGE, EDGE), :] = jnp.zeros((EDGE, width), BF16)
            px[pl.ds(rows + EDGE, EDGE), :] = jnp.zeros((EDGE, width), BF16)

    def reverse_values(wing_index, source, column, k, map_t):
        at = pl.multiple_of(k * Q, Q)
        here_columns = slice(wing_index * wing, wing_index * wing + wing)
        window = source[pl.ds(EDGE + at, Q + EDGE), column : column + wing].astype(F32)
        value = silu(taps(window, weights_r[wing_index], [3, 2, 1, 0]))
        xr[wing_index, pl.ds(at, Q), :] = value
        steps = ff[pl.ds(pl.multiple_of(k * 8, 8), 8), :]
        scaled = (value * spread(steps, select_r[:, here_columns])).astype(BF16)
        xsr[wing_index, k] = scaled
        ur[wing_index, k] = dot(map_t, scaled)

    def reverse_total(wing_index):
        def step(i, state):
            k = chunks - 1 - i
            e = exr[pl.ds(k, 1), :][:, wing_index * wing : wing_index * wing + wing]
            return e * (e * state + ur[wing_index, k])

        tot_r[wing_index] = lax.fori_loop(0, chunks // 4, by(4, step), jnp.zeros((Q, wing), F32))

    def step_maps(k, _):
        at = pl.multiple_of(k * Q, Q)
        window = pb[pl.ds(EDGE + at, Q + EDGE), :Q].astype(F32)
        map_t = silu(taps(window, weights_s[:, :Q], [3, 2, 1, 0])).T.astype(BF16)
        btr[pl.ds(at, Q), :] = map_t
        reverse_values(1, px, wing, k, map_t)
        return 0

    def step_forward(k, state):
        at = pl.multiple_of(k * Q, Q)
        window = pb[pl.ds(at, Q + 2 * EDGE), :].astype(F32)
        cr = silu(taps(window[:, Q:], weights_s[:, Q:], [EDGE + 3, EDGE + 2, EDGE + 1, EDGE])).astype(BF16)
        gcr[pl.ds(at, Q), Q:] = cr
        gcr[pl.ds(at, Q), :Q] = jnp.where(r <= c, dot(cr, btr[pl.ds(at, Q), :]), 0.0).astype(BF16)
        fwd = silu(taps(window, weights_s, [EDGE - 3, EDGE - 2, EDGE - 1, EDGE]))
        bf, cf = fwd[:, :Q].astype(BF16), fwd[:, Q:].astype(BF16)
        gcf[pl.ds(at, Q), Q:] = cf
        gcf[pl.ds(at, Q), :Q] = jnp.where(r >= c, dot_nt(cf, bf), 0.0).astype(BF16)
        window = px[pl.ds(at, Q + EDGE), :].astype(F32)
        value = silu(taps(window, weights_x, [EDGE - 3, EDGE - 2, EDGE - 1, EDGE]))
        xf[pl.ds(at, Q), :] = value
        scaled = (value * spread(ff[pl.ds(pl.multiple_of(k * 8, 8), 8), :], select_f)).astype(BF16)
        xsf[k] = scaled
        uf[k] = dot(fwd[:, :Q].T.astype(BF16), scaled)
        return state

    def forward_total(k, state):
        e = exf[pl.ds(k, 1), :]
        return e * (e * state + uf[k])

    tot = (tot_f, tot_r.at[0], tot_r.at[1])
    got = (got_f, got_r.at[0], got_r.at[1])
    inc = (inc_f, inc_r.at[0], inc_r.at[1])
    into = (in_f, in_r.at[0], in_r.at[1])

    def to_owner(way, d):
        peer = (here + d) & (seqs - 1)
        return pltpu.make_async_remote_copy(
            src_ref=tot[way].at[pl.ds(pl.multiple_of(peer * share, share), share)],
            dst_ref=got[way].at[here], send_sem=a_send.at[way], recv_sem=a_recv.at[way],
            device_id={"seq": peer, "head": mine}, device_id_type=MESH,
        )

    def from_owner(way, d):
        peer = (here + d) & (seqs - 1)
        return pltpu.make_async_remote_copy(
            src_ref=inc[way].at[peer],
            dst_ref=into[way].at[pl.ds(pl.multiple_of(here * share, share), share)],
            send_sem=b_send.at[way], recv_sem=b_recv.at[way],
            device_id={"seq": peer, "head": mine}, device_id_type=MESH,
        )

    mine_rows = pl.ds(pl.multiple_of(here * share, share), share)

    def others(buffer, sem):
        span = buffer.at[pl.ds(0, seqs - 1)]
        pltpu.make_async_copy(span, span, sem).wait()

    def states_out(way):
        def go(d, _):
            to_owner(way, d).start()
            return 0

        lax.fori_loop(1, seqs, go, 0)
        got[way][here] = tot[way][mine_rows, :]

    left = iota((1, Q), 1) < Q // 2

    def states_back(way):
        others(got[way], a_recv.at[way])
        heads = ((0, 1, 2, 3), (4, 5), (6, 7))[way]

        def hop(i, entering):
            at = i if way == 0 else seqs - 1 - i
            inc[way][at] = entering
            d = [dall[at, h : h + 1, :] for h in heads]
            decay = jnp.concatenate([jnp.where(left, d[i], d[i + 1]) for i in range(0, len(d), 2)], axis=1)
            return decay * entering + got[way][at]

        lax.fori_loop(0, seqs, hop, jnp.zeros(got[way].shape[1:], F32))

        def go(d, _):
            from_owner(way, d).start()
            return 0

        lax.fori_loop(1, seqs, go, 0)
        into[way][mine_rows, :] = inc[way][here]

    def states_in(way):
        others(inc[way], b_recv.at[way])

    each = chunks // PIECES

    def pieces(start, stop):
        def one(i, _):
            p = PIECES - 1 - i
            piece(p).wait_recv()

            for j in range(each):
                k = p * each + each - 1 - j
                reverse_values(0, pm, 0, k, btr[pl.ds(pl.multiple_of(k * Q, Q), Q), :])
            return 0

        lax.fori_loop(start, stop, one, 0)

    def rebound(p):
        at = pl.multiple_of(p * length, length)
        return pltpu.make_async_remote_copy(
            src_ref=away.at[pl.ds(at, length)], dst_ref=back_in.at[pl.ds(at, length)],
            send_sem=out_send.at[p], recv_sem=out_recv.at[p],
            device_id={"seq": here, "head": mate}, device_id_type=MESH,
        )

    def finish_reverse(wing_index, k, state):
        at = pl.multiple_of(k * Q, Q)
        here_columns = slice(wing_index * wing, wing_index * wing + wing)
        e = exr[pl.ds(k, 1), :][:, here_columns]
        entering = e * state
        y = dot(gcr[pl.ds(at, Q), :], jnp.concatenate([xsr[wing_index, k], entering.astype(BF16)], axis=0))
        scale = spread(ef[pl.ds(pl.multiple_of(k * 8, 8), 8), :], select_r[:, here_columns])
        skip = gain_r[:, here_columns] * xr[wing_index, pl.ds(at, Q), :]
        return (scale * y + skip).astype(BF16), e * (entering + ur[wing_index, k])

    def finish_away(i, state):
        p = PIECES - 1 - i
        for j in range(each):
            k = p * each + each - 1 - j
            rounded, state = finish_reverse(1, k, state)
            away[pl.ds(pl.multiple_of(k * Q, Q), Q), :] = rounded
        rebound(p).start()
        return state

    def finish_forward(k, state):
        at = pl.multiple_of(k * Q, Q)
        e = exf[pl.ds(k, 1), :]
        entering = e * state
        y = dot(gcf[pl.ds(at, Q), :], jnp.concatenate([xsf[k], entering.astype(BF16)], axis=0))
        scale = spread(ef[pl.ds(pl.multiple_of(k * 8, 8), 8), :], select_f)
        yf[pl.ds(at, Q), :] = scale * y + gain_f * xf[pl.ds(at, Q), :]
        return e * (entering + uf[k])

    def finish_home(i, state):
        for j in range(4):
            k = chunks - 1 - 4 * i - j
            at = pl.multiple_of(k * Q, Q)
            rounded, state = finish_reverse(0, k, state)
            out_ref[pl.ds(at, Q), :wing] = (yf[pl.ds(at, Q), :wing] + rounded.astype(F32)).astype(BF16)
        return state

    def add_returned(i, _):
        p = PIECES - 1 - i
        rebound(p).wait_recv()
        at = pl.ds(pl.multiple_of(p * length, length), length)
        out_ref[at, wing:] = (yf[at, wing:] + back_in[at, :].astype(F32)).astype(BF16)
        return 0

    lax.fori_loop(0, chunks // 4 - 1, by(4, step_maps), 0)
    arrive_halos()
    lax.fori_loop(chunks // 4 - 1, chunks // 4, by(4, step_maps), 0)
    reverse_total(1)
    states_out(2)
    lax.fori_loop(0, chunks // 4, by(4, step_forward), 0)
    tot_f[...] = lax.fori_loop(0, chunks // 4, by(4, forward_total), jnp.zeros((Q, width), F32))
    states_out(0)
    everyone = dall.at[pl.ds(0, seqs - 1)]
    pltpu.make_async_copy(everyone, everyone, d_recv).wait()
    states_back(2)
    halos[4].wait_recv()

    @pl.when(here == seqs - 1)
    def _():
        pm[pl.ds(rows + EDGE, EDGE), :] = jnp.zeros((EDGE, wing), BF16)

    pieces(0, PIECES)
    reverse_total(0)
    states_out(1)
    states_back(0)
    states_in(2)
    lax.fori_loop(0, PIECES, finish_away, in_r[1])
    states_back(1)
    states_in(0)
    lax.fori_loop(0, chunks // 4, by(4, finish_forward), in_f[...])
    states_in(1)
    lax.fori_loop(0, chunks // 4, finish_home, in_r[0])
    lax.fori_loop(0, PIECES, add_returned, 0)

    for copy in halos:
        copy.wait_send()

    for p in range(PIECES):
        piece(p).wait_send()
        rebound(p).wait_send()

    pltpu.make_async_copy(everyone, everyone, d_send).wait()
    for way in range(3):
        others(got[way], a_send.at[way])
        others(inc[way], b_send.at[way])


def per_device(inputs, bc_inputs, dt_raw, conv_inner, conv_state, log_rate, dt_bias, skip_gain):
    seqs, ways = lax.axis_size("seq"), lax.axis_size("head")
    rows, width = inputs.shape
    chunks, share, wing = rows // Q, Q // seqs, width // 2
    anywhere = pl.BlockSpec(memory_space=pl.ANY)
    vmem = pl.BlockSpec(memory_space=pltpu.VMEM)
    padded = pltpu.VMEM((rows + 2 * EDGE, width), BF16)
    dma = pltpu.SemaphoreType.DMA
    return pl.pallas_call(
        functools.partial(kernel, seqs, ways),
        out_shape=jax.ShapeDtypeStruct((rows, width), BF16),
        in_specs=[anywhere] * 4 + [vmem] * 4,
        out_specs=vmem,
        scratch_shapes=[
            pltpu.VMEM(dt_raw.shape, BF16), pltpu.VMEM((4, width), F32), pltpu.VMEM((4, wing), F32),
            padded, padded, pltpu.VMEM((rows + 2 * EDGE, wing), BF16),
            pltpu.VMEM((rows, 2 * Q), BF16), pltpu.VMEM((rows, 2 * Q), BF16), pltpu.VMEM((rows, Q), BF16),
            pltpu.VMEM((chunks, Q, width), BF16), pltpu.VMEM((2, chunks, Q, wing), BF16),
            pltpu.VMEM((rows, width), F32), pltpu.VMEM((2, rows, wing), F32),
            pltpu.VMEM((chunks, Q, width), F32), pltpu.VMEM((2, chunks, Q, wing), F32),
            pltpu.VMEM((rows, width), F32),
            pltpu.VMEM((chunks * 8, Q), F32), pltpu.VMEM((chunks * 8, Q), F32),
            pltpu.VMEM((chunks, width), F32), pltpu.VMEM((chunks, width), F32),
            pltpu.VMEM((rows, wing), BF16), pltpu.VMEM((rows, wing), BF16),
            pltpu.VMEM((Q, width), F32), pltpu.VMEM((2, Q, wing), F32),
            pltpu.VMEM((seqs, share, width), F32), pltpu.VMEM((2, seqs, share, wing), F32),
            pltpu.VMEM((seqs, share, width), F32), pltpu.VMEM((2, seqs, share, wing), F32),
            pltpu.VMEM((Q, width), F32), pltpu.VMEM((2, Q, wing), F32),
            pltpu.VMEM((8, Q), F32), pltpu.VMEM((seqs, 8, Q), F32),
            dma((5,)), dma((5,)), dma((5,)), dma((PIECES,)), dma((PIECES,)), dma((PIECES,)), dma((PIECES,)),
            dma, dma, dma((3,)), dma((3,)), dma((3,)), dma((3,)),
        ],
        compiler_params=pltpu.CompilerParams(
            collective_id=0, has_side_effects=True, vmem_limit_bytes=60 * 2**20
        ),
    )(
        inputs, bc_inputs, dt_raw, conv_inner, conv_state,
        log_rate[None, :], dt_bias[None, :], skip_gain[None, :],
    )


def solution(mesh):
    return jax.shard_map(
        per_device,
        mesh=mesh,
        in_specs=(P("seq", "head"), P("seq", None), P(None, "seq"), P(), P(), P(), P(), P()),
        out_specs=P("seq", "head"),
        check_vma=False,
    )
```

```python
import functools

import jax
import jax.numpy as jnp
from jax import lax
from jax.experimental import pallas as pl
from jax.experimental.pallas import tpu as pltpu
from jax.sharding import PartitionSpec as P

Q = 128
EDGE = 16
HEADS = 4
PIECES = 8
TAIL = 2
HIGHEST = lax.Precision.HIGHEST
MESH = pl.DeviceIdType.MESH
F32 = jnp.float32
BF16 = jnp.bfloat16


def iota(shape, dim):
    return lax.broadcasted_iota(jnp.int32, shape, dim)


def silu(v):
    h = 0.5 * v
    return h * jnp.tanh(h) + h


def taps(window, weights, begins):
    total = weights[0:1, :] * window[begins[0] : begins[0] + Q]
    for i in range(1, 4):
        total = total + weights[i : i + 1, :] * window[begins[i] : begins[i] + Q]
    return total


def dot(a, b):
    return jnp.dot(a, b, preferred_element_type=F32)


def dot_nt(a, b):
    return lax.dot_general(a, b, (((1,), (1,)), ((), ())), preferred_element_type=F32)


def spread(rows, select):
    high = rows.astype(BF16).astype(F32)
    parts = jnp.concatenate([high, rows - high], axis=0)
    return dot(parts.T.astype(BF16), select)


def kernel(
    seqs, ways,
    x_hbm, bc_hbm, dt_hbm, wx_hbm, ws_ref, rate_ref, bias_ref, gain_ref,
    out_ref,
    dt_ref, wx_ref, wm_ref, px, pb, pm, gcf, gcr, btr, xsf, xsr, xf, xr, uf, ur, yf, ef, ff, er, fr, exf, exm, exr,
    back, tot_f, tot_r, got_f, got_r, inc_f, inc_r, in_f, in_r, dmsg, dall,
    local_sem, halo_send, halo_recv, piece_send, piece_recv,
    d_send, d_recv, a_send, a_recv, b_send, b_recv,
):
    rows, width = x_hbm.shape
    chunks = rows // Q
    share = Q // seqs
    wing = width // 2
    here, mine = lax.axis_index("seq"), lax.axis_index("head")
    mate = (mine + ways // 2) & (ways - 1)
    after, before = (here + 1) & (seqs - 1), (here - 1) & (seqs - 1)

    own_x = pltpu.make_async_copy(x_hbm, px.at[pl.ds(EDGE, rows)], local_sem.at[0])
    own_bc = pltpu.make_async_copy(bc_hbm, pb.at[pl.ds(EDGE, rows)], local_sem.at[1])
    own_dt = pltpu.make_async_copy(dt_hbm, dt_ref, local_sem.at[2])
    columns = pl.ds(pl.multiple_of(mine * width, width), width)
    theirs = pl.ds(pl.multiple_of(mate * width, width), width)
    mate_w = pltpu.make_async_copy(wx_hbm.at[:, theirs], wm_ref, local_sem.at[4])
    own_w = pltpu.make_async_copy(wx_hbm.at[:, columns], wx_ref, local_sem.at[3])

    barrier = pltpu.get_barrier_semaphore()

    def greet(d, _):
        peer = (here + d) & (seqs - 1)
        pl.semaphore_signal(barrier, inc=1, device_id={"seq": peer, "head": mine}, device_id_type=MESH)
        return 0

    def greet_mate(d, _):
        peer = (here + d) & (seqs - 1)
        pl.semaphore_signal(barrier, inc=1, device_id={"seq": peer, "head": mate}, device_id_type=MESH)
        return 0

    lax.fori_loop(1, seqs, greet, 0)
    lax.fori_loop(0, seqs, greet_mate, 0)
    own_dt.start()
    own_bc.start()
    own_x.start()
    own_w.start()
    mate_w.start()
    pl.semaphore_wait(barrier, 2 * seqs - 1)

    def halo(i, src, dst, s, h):
        return pltpu.make_async_remote_copy(
            src_ref=src, dst_ref=dst, send_sem=halo_send.at[i], recv_sem=halo_recv.at[i],
            device_id={"seq": s, "head": h}, device_id_type=MESH,
        )

    first, last = pl.ds(0, EDGE), pl.ds(rows - EDGE, EDGE)
    low, high = pl.ds(0, EDGE), pl.ds(rows + EDGE, EDGE)
    halos = [
        halo(0, bc_hbm.at[last], pb.at[low], after, mine),
        halo(1, bc_hbm.at[first], pb.at[high], before, mine),
        halo(2, x_hbm.at[last], px.at[low], after, mine),
        halo(3, x_hbm.at[first], px.at[high], before, mine),
        halo(4, x_hbm.at[first], pm.at[high], before, mate),
    ]
    for copy in halos:
        copy.start()
    length = rows // PIECES

    def piece(p):
        at = pl.multiple_of(p * length, length)
        return pltpu.make_async_remote_copy(
            src_ref=x_hbm.at[pl.ds(at, length)], dst_ref=pm.at[pl.ds(EDGE + at, length)],
            send_sem=piece_send.at[p], recv_sem=piece_recv.at[p],
            device_id={"seq": here, "head": mate}, device_id_type=MESH,
        )

    def push(i, _):
        piece(PIECES - 1 - i).start()
        return 0

    lax.fori_loop(0, 6, push, 0)

    own_dt.wait()

    all_heads = dt_ref.shape[0]
    row8, head8 = iota((8, all_heads), 0), iota((8, all_heads), 1)
    r, c = iota((Q, Q), 0), iota((Q, Q), 1)
    per = width // HEADS
    head_row, head_col = iota((chunks * 8, width), 0) & 7, iota((chunks * 8, width), 1) // per
    to_chunk = (iota((chunks, chunks * 8), 1) // 8 == iota((chunks, chunks * 8), 0)).astype(F32)

    def pick(owner8, values):
        return jnp.sum(jnp.where(head8 == owner8, values, 0.0), axis=1, keepdims=True)

    def stack(values):
        return jnp.concatenate([values[:, k * Q : (k + 1) * Q] for k in range(chunks)], axis=0)

    def steps_of(owner8, source8, forwards, e_ref, f_ref):
        raw8 = dot((head8 == source8).astype(F32).astype(BF16), dt_ref[...])
        rate8 = pick(owner8, -jnp.exp(rate_ref[...]))
        pre = raw8 + pick(owner8, bias_ref[...])
        dt8 = jnp.maximum(pre, 0.0) + jnp.log1p(jnp.exp(-jnp.abs(pre)))
        logs = stack(dt8 * rate8)
        cum = jnp.dot(logs, (r >= c).astype(F32), precision=HIGHEST, preferred_element_type=F32)
        if forwards:
            upto = jnp.dot(logs, (r <= c).astype(F32), precision=HIGHEST, preferred_element_type=F32)
            cum = jnp.where((iota((chunks * 8, Q), 0) & 7) < forwards, upto, cum)
        half = 0.5 * jnp.sum(logs, axis=1, keepdims=True)
        e_ref[...] = jnp.exp(cum - half)
        f_ref[...] = stack(dt8) * jnp.exp(half - cum)
        return half

    def chunk_decay(half, offset):
        wide = jnp.where(head_row == head_col + offset, half, 0.0)
        return jnp.exp(jnp.dot(to_chunk, wide, precision=HIGHEST, preferred_element_type=F32))

    local = row8 & (HEADS - 1)
    own8 = mine * HEADS + local
    half = steps_of(jnp.where(row8 < HEADS, mine, mate) * HEADS + local, own8, HEADS, ef, ff)
    exf[...] = chunk_decay(half, 0)
    exm[...] = chunk_decay(half, HEADS)
    gain = jnp.sum(
        jnp.where(iota((8, width), 0) == iota((8, width), 1) // per, pick(own8, gain_ref[...]), 0.0),
        axis=0, keepdims=True,
    )
    sel_row, sel_col = iota((16, width), 0) & 7, iota((16, width), 1) // per
    select_f = (sel_row == sel_col).astype(F32).astype(BF16)
    select_r = (sel_row == sel_col + HEADS).astype(F32).astype(BF16)
    all_logs = sum(half[8 * k : 8 * k + 8, :] for k in range(chunks))
    decay = jnp.broadcast_to(jnp.exp(2.0 * all_logs), (8, Q))
    dmsg[...] = decay
    dall[here] = decay

    def tell(d):
        return pltpu.make_async_remote_copy(
            src_ref=dmsg, dst_ref=dall.at[here], send_sem=d_send, recv_sem=d_recv,
            device_id={"seq": (here + d) & (seqs - 1), "head": mine}, device_id_type=MESH,
        )

    def tell_start(d, _):
        tell(d).start()
        return 0

    lax.fori_loop(1, seqs, tell_start, 0)

    own_w.wait()
    mate_w.wait()
    weights_x = wx_ref[...]
    weights_m = wm_ref[...]
    weights_s = ws_ref[...]

    own_x.wait()
    own_bc.wait()
    def by(n, body):
        def several(i, state):
            for j in range(n):
                state = body(n * i + j, state)
            return state

        return several

    def arrive_halos():
        for i in range(4):
            halos[i].wait_recv()

        @pl.when(here == 0)
        def _():
            px[pl.ds(0, EDGE), :] = jnp.zeros((EDGE, width), BF16)
            pb[pl.ds(0, EDGE), :] = jnp.zeros((EDGE, width), BF16)

        @pl.when(here == seqs - 1)
        def _():
            pb[pl.ds(rows + EDGE, EDGE), :] = jnp.zeros((EDGE, width), BF16)
            px[pl.ds(rows + EDGE, EDGE), :] = jnp.zeros((EDGE, width), BF16)

    def reverse_total():
        def step(i, state):
            k = chunks - 1 - i
            e = exm[pl.ds(k, 1), :]
            return e * (e * state + ur[k])

        tot_r[...] = lax.fori_loop(0, chunks // 4, by(4, step), jnp.zeros((Q, width), F32))

    def step_mate(k, _):
        at = pl.multiple_of(k * Q, Q)
        window = pb[pl.ds(EDGE + at, Q + EDGE), :Q].astype(F32)
        map_t = silu(taps(window, weights_s[:, :Q], [3, 2, 1, 0])).T.astype(BF16)
        btr[pl.ds(at, Q), :] = map_t
        window = px[pl.ds(EDGE + at, Q + EDGE), :].astype(F32)
        value = silu(taps(window, weights_m, [3, 2, 1, 0]))
        scaled = value * spread(ff[pl.ds(pl.multiple_of(k * 8, 8), 8), :], select_r)
        ur[k] = dot(map_t, scaled.astype(BF16))
        return 0

    def step_maps(k, _):
        at = pl.multiple_of(k * Q, Q)
        window = pb[pl.ds(EDGE + at, Q + EDGE), Q:].astype(F32)
        cr = silu(taps(window, weights_s[:, Q:], [3, 2, 1, 0])).astype(BF16)
        gcr[pl.ds(at, Q), Q:] = cr
        gcr[pl.ds(at, Q), :Q] = jnp.where(r <= c, dot(cr, btr[pl.ds(at, Q), :]), 0.0).astype(BF16)
        return 0

    def step_reverse(k):
        at = pl.multiple_of(k * Q, Q)
        window = pm[pl.ds(EDGE + at, Q + EDGE), :].astype(F32)
        value = silu(taps(window, weights_x, [3, 2, 1, 0]))
        xr[pl.ds(at, Q), :] = value
        scaled = (value * spread(fr[pl.ds(pl.multiple_of(k * 8, 8), 8), :], select_f)).astype(BF16)
        xsr[k] = scaled
        ur[k] = dot(btr[pl.ds(at, Q), :], scaled)

    def step_forward(k, state):
        at = pl.multiple_of(k * Q, Q)
        window = pb[pl.ds(at, Q + EDGE), :].astype(F32)
        fwd = silu(taps(window, weights_s, [EDGE - 3, EDGE - 2, EDGE - 1, EDGE]))
        bf, cf = fwd[:, :Q].astype(BF16), fwd[:, Q:].astype(BF16)
        gcf[pl.ds(at, Q), Q:] = cf
        gcf[pl.ds(at, Q), :Q] = jnp.where(r >= c, dot_nt(cf, bf), 0.0).astype(BF16)
        window = px[pl.ds(at, Q + EDGE), :].astype(F32)
        value = silu(taps(window, weights_x, [EDGE - 3, EDGE - 2, EDGE - 1, EDGE]))
        xf[pl.ds(at, Q), :] = value
        scaled = (value * spread(ff[pl.ds(pl.multiple_of(k * 8, 8), 8), :], select_f)).astype(BF16)
        xsf[k] = scaled
        uf[k] = dot(fwd[:, :Q].T.astype(BF16), scaled)
        return state

    def forward_total(k, state):
        e = exf[pl.ds(k, 1), :]
        return e * (e * state + uf[k])

    tot, got, inc = (tot_f, tot_r), (got_f, got_r), (inc_f, inc_r)

    def to_owner(way, d):
        peer = (here + d) & (seqs - 1)
        return pltpu.make_async_remote_copy(
            src_ref=tot[way].at[pl.ds(pl.multiple_of(peer * share, share), share)],
            dst_ref=got[way].at[here], send_sem=a_send.at[way], recv_sem=a_recv.at[way],
            device_id={"seq": peer, "head": mine}, device_id_type=MESH,
        )

    def from_owner(way, d):
        peer = (here + d) & (seqs - 1)
        landing = in_f.at[pl.ds(pl.multiple_of(here * share, share), share)] if way == 0 else in_r.at[here]
        return pltpu.make_async_remote_copy(
            src_ref=inc[way].at[peer], dst_ref=landing,
            send_sem=b_send.at[way], recv_sem=b_recv.at[way],
            device_id={"seq": peer, "head": mine if way == 0 else mate}, device_id_type=MESH,
        )

    mine_rows = pl.ds(pl.multiple_of(here * share, share), share)

    def others(buffer, sem, count=seqs - 1):
        span = buffer.at[pl.ds(0, count)]
        pltpu.make_async_copy(span, span, sem).wait()

    def states_out(way):
        def go(d, _):
            to_owner(way, d).start()
            return 0

        lax.fori_loop(1, seqs, go, 0)
        got[way][here] = tot[way][mine_rows, :]

    left = iota((1, Q), 1) < Q // 2

    def states_back(way):
        others(got[way], a_recv.at[way])

        def hop(i, entering):
            at = i if way == 0 else seqs - 1 - i
            if way == 0:
                inc_f[at] = entering
            else:
                inc_r[at] = jnp.concatenate([entering[:, :wing], entering[:, wing:]], axis=0).astype(BF16)
            d = [dall[at, HEADS * way + h : HEADS * way + h + 1, :] for h in range(HEADS)]
            decay = jnp.concatenate([jnp.where(left, d[0], d[1]), jnp.where(left, d[2], d[3])], axis=1)
            return decay * entering + got[way][at]

        lax.fori_loop(0, seqs, hop, jnp.zeros(got[way].shape[1:], F32))

        def go(d, _):
            from_owner(way, d).start()
            return 0

        lax.fori_loop(1 - way, seqs, go, 0)
        if way == 0:
            in_f[mine_rows, :] = inc_f[here]

    def entered():
        others(in_r, b_recv.at[1], seqs)
        blocks = [in_r[j].astype(F32) for j in range(seqs)]
        return jnp.concatenate([jnp.concatenate([b[:share], b[share:]], axis=1) for b in blocks], axis=0)

    each = chunks // PIECES

    def pieces(start, stop):
        def one(i, _):
            p = PIECES - 1 - i
            piece(p).wait_recv()

            for j in range(each):
                k = p * each + each - 1 - j
                step_reverse(k)
            return 0

        lax.fori_loop(start, stop, one, 0)

    def finish_forward(k, state, early):
        at = pl.multiple_of(k * Q, Q)
        e = exf[pl.ds(k, 1), :]
        entering = e * state
        y = dot(gcf[pl.ds(at, Q), :], jnp.concatenate([xsf[k], entering.astype(BF16)], axis=0))
        scale = spread(ef[pl.ds(pl.multiple_of(k * 8, 8), 8), :], select_f)
        y = scale * y + gain * xf[pl.ds(at, Q), :]
        if early:
            out_ref[pl.ds(at, Q), :] = (y + back[pl.ds(at, Q), :].astype(F32)).astype(BF16)
        else:
            yf[pl.ds(at, Q), :] = y
        return e * (entering + uf[k])

    def finish_reverse(k, state):
        at = pl.multiple_of(k * Q, Q)
        e = exr[pl.ds(k, 1), :]
        entering = e * state
        y = dot(gcr[pl.ds(at, Q), :], jnp.concatenate([xsr[k], entering.astype(BF16)], axis=0))
        scale = spread(er[pl.ds(pl.multiple_of(k * 8, 8), 8), :], select_f)
        return (scale * y + gain * xr[pl.ds(at, Q), :]).astype(BF16), e * (entering + ur[k])

    def finish_early(i, state):
        k = chunks - 1 - i
        back[pl.ds(pl.multiple_of(k * Q, Q), Q), :], state = finish_reverse(k, state)
        return state

    late = TAIL * each

    lax.fori_loop(0, chunks // 4 - 1, by(4, step_mate), 0)
    arrive_halos()
    lax.fori_loop(chunks // 4 - 1, chunks // 4, by(4, step_mate), 0)
    reverse_total()
    states_out(1)
    lax.fori_loop(0, chunks // 4, by(4, step_forward), 0)
    tot_f[...] = lax.fori_loop(0, chunks // 4, by(4, forward_total), jnp.zeros((Q, width), F32))
    states_out(0)
    lax.fori_loop(0, chunks // 4, by(4, step_maps), 0)
    half = steps_of(own8, mate * HEADS + local, 0, er, fr)
    exr[...] = chunk_decay(half, 0)
    everyone = dall.at[pl.ds(0, seqs - 1)]
    pltpu.make_async_copy(everyone, everyone, d_recv).wait()
    states_back(1)
    lax.fori_loop(6, PIECES, push, 0)
    halos[4].wait_recv()

    @pl.when(here == seqs - 1)
    def _():
        pm[pl.ds(rows + EDGE, EDGE), :] = jnp.zeros((EDGE, width), BF16)

    pieces(0, PIECES // 2)
    states_back(0)
    pieces(PIECES // 2, PIECES - TAIL)
    state = lax.fori_loop(0, (chunks - late) // 4, by(4, finish_early), entered())
    others(inc_f, b_recv.at[0])
    forward = lax.fori_loop(0, late // 4, by(4, lambda k, st: finish_forward(k, st, False)), in_f[...])
    lax.fori_loop(late // 4, chunks // 4, by(4, lambda k, st: finish_forward(k, st, True)), forward)

    def finish_late(i, state):
        p = TAIL - 1 - i
        piece(p).wait_recv()
        ks = [p * each + each - 1 - j for j in range(each)]
        for k in ks:
            step_reverse(k)
        for k in ks:
            at = pl.multiple_of(k * Q, Q)
            rounded, state = finish_reverse(k, state)
            out_ref[pl.ds(at, Q), :] = (yf[pl.ds(at, Q), :] + rounded.astype(F32)).astype(BF16)
        return state

    lax.fori_loop(0, TAIL, finish_late, state)

    for copy in halos:
        copy.wait_send()

    for p in range(PIECES):
        piece(p).wait_send()

    pltpu.make_async_copy(everyone, everyone, d_send).wait()
    for way in (0, 1):
        others(got[way], a_send.at[way])
        others(inc[way], b_send.at[way], seqs - 1 + way)


def per_device(inputs, bc_inputs, dt_raw, conv_inner, conv_state, log_rate, dt_bias, skip_gain):
    seqs, ways = lax.axis_size("seq"), lax.axis_size("head")
    rows, width = inputs.shape
    chunks, share, wing = rows // Q, Q // seqs, width // 2
    anywhere = pl.BlockSpec(memory_space=pl.ANY)
    vmem = pl.BlockSpec(memory_space=pltpu.VMEM)
    padded = pltpu.VMEM((rows + 2 * EDGE, width), BF16)
    steps, decays = pltpu.VMEM((chunks * 8, Q), F32), pltpu.VMEM((chunks, width), F32)
    dma = pltpu.SemaphoreType.DMA
    return pl.pallas_call(
        functools.partial(kernel, seqs, ways),
        out_shape=jax.ShapeDtypeStruct((rows, width), BF16),
        in_specs=[anywhere] * 4 + [vmem] * 4,
        out_specs=vmem,
        scratch_shapes=[
            pltpu.VMEM(dt_raw.shape, BF16), pltpu.VMEM((4, width), F32), pltpu.VMEM((4, width), F32),
            padded, padded, padded,
            pltpu.VMEM((rows, 2 * Q), BF16), pltpu.VMEM((rows, 2 * Q), BF16), pltpu.VMEM((rows, Q), BF16),
            pltpu.VMEM((chunks, Q, width), BF16), pltpu.VMEM((chunks, Q, width), BF16),
            pltpu.VMEM((rows, width), F32), pltpu.VMEM((rows, width), F32),
            pltpu.VMEM((chunks, Q, width), F32), pltpu.VMEM((chunks, Q, width), F32),
            pltpu.VMEM((rows, width), F32),
            steps, steps, steps, steps, decays, decays, decays,
            pltpu.VMEM((rows, width), BF16), pltpu.VMEM((Q, width), F32), pltpu.VMEM((Q, width), F32),
            pltpu.VMEM((seqs, share, width), F32), pltpu.VMEM((seqs, share, width), F32),
            pltpu.VMEM((seqs, share, width), F32), pltpu.VMEM((seqs, 2 * share, wing), BF16),
            pltpu.VMEM((Q, width), F32), pltpu.VMEM((seqs, 2 * share, wing), BF16),
            pltpu.VMEM((8, Q), F32), pltpu.VMEM((seqs, 8, Q), F32),
            dma((5,)), dma((5,)), dma((5,)), dma((PIECES,)), dma((PIECES,)),
            dma, dma, dma((2,)), dma((2,)), dma((2,)), dma((2,)),
        ],
        compiler_params=pltpu.CompilerParams(
            collective_id=0, has_side_effects=True, vmem_limit_bytes=60 * 2**20
        ),
    )(
        inputs, bc_inputs, dt_raw, conv_inner, conv_state,
        log_rate[None, :], dt_bias[None, :], skip_gain[None, :],
    )


def solution(mesh):
    return jax.shard_map(
        per_device,
        mesh=mesh,
        in_specs=(P("seq", "head"), P("seq", None), P(None, "seq"), P(), P(), P(), P(), P()),
        out_specs=P("seq", "head"),
        check_vma=False,
    )
```

```python
import functools

import jax
import jax.numpy as jnp
from jax import lax
from jax.experimental import pallas as pl
from jax.experimental.pallas import tpu as pltpu
from jax.sharding import PartitionSpec as P

Q = 128
EDGE = 16
HEADS = 4
PIECES = 8
TAIL = 2
HIGHEST = lax.Precision.HIGHEST
MESH = pl.DeviceIdType.MESH
F32 = jnp.float32
BF16 = jnp.bfloat16


def iota(shape, dim):
    return lax.broadcasted_iota(jnp.int32, shape, dim)


def silu(v):
    h = 0.5 * v
    return h * jnp.tanh(h) + h


def taps(window, weights, begins):
    total = weights[0:1, :] * window[begins[0] : begins[0] + Q]
    for i in range(1, 4):
        total = total + weights[i : i + 1, :] * window[begins[i] : begins[i] + Q]
    return total


def dot(a, b):
    return jnp.dot(a, b, preferred_element_type=F32)


def dot_nt(a, b):
    return lax.dot_general(a, b, (((1,), (1,)), ((), ())), preferred_element_type=F32)


def spread(rows, select):
    high = rows.astype(BF16).astype(F32)
    parts = jnp.concatenate([high, rows - high], axis=0)
    return dot(parts.T.astype(BF16), select)


def kernel(
    seqs, ways,
    x_hbm, bc_hbm, dt_hbm, wx_hbm, ws_hbm, rate_hbm, bias_hbm, gain_hbm,
    out_ref,
    ws_ref, rate_ref, bias_ref, gain_ref, dt_ref, wx_ref, wm_ref, px, pb, pm, gcf, gcr, btr, btf, xsf, xsr, xf, xr, uf, ur, yf, ef, ff, er, fr, exf, exm, exr,
    back, tot_f, tot_r, got_f, got_r, inc_f, inc_r, in_f, in_r, dmsg, dall,
    local_sem, halo_send, halo_recv, piece_send, piece_recv,
    d_send, d_recv, a_send, a_recv, b_send, b_recv,
):
    rows, width = x_hbm.shape
    chunks = rows // Q
    share = Q // seqs
    wing = width // 2
    here, mine = lax.axis_index("seq"), lax.axis_index("head")
    mate = (mine + ways // 2) & (ways - 1)
    after, before = (here + 1) & (seqs - 1), (here - 1) & (seqs - 1)

    own_x = pltpu.make_async_copy(x_hbm, px.at[pl.ds(EDGE, rows)], local_sem.at[0])
    own_bc = pltpu.make_async_copy(bc_hbm, pb.at[pl.ds(EDGE, rows)], local_sem.at[1])
    own_dt = pltpu.make_async_copy(dt_hbm, dt_ref, local_sem.at[2])
    columns = pl.ds(pl.multiple_of(mine * width, width), width)
    theirs = pl.ds(pl.multiple_of(mate * width, width), width)
    mate_w = pltpu.make_async_copy(wx_hbm.at[:, theirs], wm_ref, local_sem.at[4])
    own_w = pltpu.make_async_copy(wx_hbm.at[:, columns], wx_ref, local_sem.at[3])

    barrier = pltpu.get_barrier_semaphore()

    def greet(d, _):
        peer = (here + d) & (seqs - 1)
        pl.semaphore_signal(barrier, inc=1, device_id={"seq": peer, "head": mine}, device_id_type=MESH)
        return 0

    def greet_mate(d, _):
        peer = (here + d) & (seqs - 1)
        pl.semaphore_signal(barrier, inc=1, device_id={"seq": peer, "head": mate}, device_id_type=MESH)
        return 0

    lax.fori_loop(1, seqs, greet, 0)
    lax.fori_loop(0, seqs, greet_mate, 0)
    small = [
        pltpu.make_async_copy(source, target, local_sem.at[5 + i])
        for i, (source, target) in enumerate(
            ((rate_hbm, rate_ref), (bias_hbm, bias_ref), (gain_hbm, gain_ref), (ws_hbm, ws_ref))
        )
    ]
    own_dt.start()
    for copy in small:
        copy.start()
    own_bc.start()
    own_x.start()
    own_w.start()
    mate_w.start()
    pl.semaphore_wait(barrier, 2 * seqs - 1)

    def halo(i, src, dst, s, h):
        return pltpu.make_async_remote_copy(
            src_ref=src, dst_ref=dst, send_sem=halo_send.at[i], recv_sem=halo_recv.at[i],
            device_id={"seq": s, "head": h}, device_id_type=MESH,
        )

    first, last = pl.ds(0, EDGE), pl.ds(rows - EDGE, EDGE)
    low, high = pl.ds(0, EDGE), pl.ds(rows + EDGE, EDGE)
    halos = [
        halo(0, bc_hbm.at[last], pb.at[low], after, mine),
        halo(1, bc_hbm.at[first], pb.at[high], before, mine),
        halo(2, x_hbm.at[last], px.at[low], after, mine),
        halo(3, x_hbm.at[first], px.at[high], before, mine),
        halo(4, x_hbm.at[first], pm.at[high], before, mate),
    ]
    for copy in halos:
        copy.start()
    length = rows // PIECES

    def piece(p):
        at = pl.multiple_of(p * length, length)
        return pltpu.make_async_remote_copy(
            src_ref=x_hbm.at[pl.ds(at, length)], dst_ref=pm.at[pl.ds(EDGE + at, length)],
            send_sem=piece_send.at[p], recv_sem=piece_recv.at[p],
            device_id={"seq": here, "head": mate}, device_id_type=MESH,
        )

    def push(i, _):
        piece(PIECES - 1 - i).start()
        return 0

    lax.fori_loop(0, 6, push, 0)

    own_dt.wait()
    for copy in small:
        copy.wait()

    all_heads = dt_ref.shape[0]
    row8, head8 = iota((8, all_heads), 0), iota((8, all_heads), 1)
    r, c = iota((Q, Q), 0), iota((Q, Q), 1)
    per = width // HEADS
    head_row, head_col = iota((chunks * 8, width), 0) & 7, iota((chunks * 8, width), 1) // per
    to_chunk = (iota((chunks, chunks * 8), 1) // 8 == iota((chunks, chunks * 8), 0)).astype(F32)

    def pick(owner8, values):
        return jnp.sum(jnp.where(head8 == owner8, values, 0.0), axis=1, keepdims=True)

    def stack(values):
        return jnp.concatenate([values[:, k * Q : (k + 1) * Q] for k in range(chunks)], axis=0)

    def steps_of(owner8, source8, forwards, e_ref, f_ref):
        raw8 = dot((head8 == source8).astype(F32).astype(BF16), dt_ref[...])
        rate8 = pick(owner8, -jnp.exp(rate_ref[...]))
        pre = raw8 + pick(owner8, bias_ref[...])
        dt8 = jnp.maximum(pre, 0.0) + jnp.log1p(jnp.exp(-jnp.abs(pre)))
        logs = stack(dt8 * rate8)
        cum = jnp.dot(logs, (r >= c).astype(F32), precision=HIGHEST, preferred_element_type=F32)
        if forwards:
            upto = jnp.dot(logs, (r <= c).astype(F32), precision=HIGHEST, preferred_element_type=F32)
            cum = jnp.where((iota((chunks * 8, Q), 0) & 7) < forwards, upto, cum)
        half = 0.5 * jnp.sum(logs, axis=1, keepdims=True)
        e_ref[...] = jnp.exp(cum - half)
        f_ref[...] = stack(dt8) * jnp.exp(half - cum)
        return half

    def chunk_decay(half, offset):
        wide = jnp.where(head_row == head_col + offset, half, 0.0)
        return jnp.exp(jnp.dot(to_chunk, wide, precision=HIGHEST, preferred_element_type=F32))

    local = row8 & (HEADS - 1)
    own8 = mine * HEADS + local
    half = steps_of(jnp.where(row8 < HEADS, mine, mate) * HEADS + local, own8, HEADS, ef, ff)
    exf[...] = chunk_decay(half, 0)
    exm[...] = chunk_decay(half, HEADS)
    gain = jnp.sum(
        jnp.where(iota((8, width), 0) == iota((8, width), 1) // per, pick(own8, gain_ref[...]), 0.0),
        axis=0, keepdims=True,
    )
    sel_row, sel_col = iota((16, width), 0) & 7, iota((16, width), 1) // per
    select_f = (sel_row == sel_col).astype(F32).astype(BF16)
    select_r = (sel_row == sel_col + HEADS).astype(F32).astype(BF16)
    all_logs = sum(half[8 * k : 8 * k + 8, :] for k in range(chunks))
    decay = jnp.broadcast_to(jnp.exp(2.0 * all_logs), (8, Q))
    dmsg[...] = decay
    dall[here] = decay

    def tell(d):
        return pltpu.make_async_remote_copy(
            src_ref=dmsg, dst_ref=dall.at[here], send_sem=d_send, recv_sem=d_recv,
            device_id={"seq": (here + d) & (seqs - 1), "head": mine}, device_id_type=MESH,
        )

    def tell_start(d, _):
        tell(d).start()
        return 0

    lax.fori_loop(1, seqs, tell_start, 0)

    own_w.wait()
    mate_w.wait()
    weights_x = wx_ref[...]
    weights_m = wm_ref[...]
    weights_s = ws_ref[...]

    own_x.wait()
    own_bc.wait()
    def by(n, body):
        def several(i, state):
            for j in range(n):
                state = body(n * i + j, state)
            return state

        return several

    def arrive_halos():
        for i in range(4):
            halos[i].wait_recv()

        @pl.when(here == 0)
        def _():
            px[pl.ds(0, EDGE), :] = jnp.zeros((EDGE, width), BF16)
            pb[pl.ds(0, EDGE), :] = jnp.zeros((EDGE, width), BF16)

        @pl.when(here == seqs - 1)
        def _():
            pb[pl.ds(rows + EDGE, EDGE), :] = jnp.zeros((EDGE, width), BF16)
            px[pl.ds(rows + EDGE, EDGE), :] = jnp.zeros((EDGE, width), BF16)

    def reverse_total():
        def step(i, state):
            k = chunks - 1 - i
            e = exm[pl.ds(k, 1), :]
            return e * (e * state + ur[k])

        tot_r[...] = lax.fori_loop(0, chunks // 4, by(4, step), jnp.zeros((Q, width), F32))

    def step_mate(k, _):
        at = pl.multiple_of(k * Q, Q)
        window = pb[pl.ds(EDGE + at, Q + EDGE), :Q].astype(F32)
        map_t = silu(taps(window, weights_s[:, :Q], [3, 2, 1, 0])).T.astype(BF16)
        btr[pl.ds(at, Q), :] = map_t
        window = px[pl.ds(EDGE + at, Q + EDGE), :].astype(F32)
        value = silu(taps(window, weights_m, [3, 2, 1, 0]))
        scaled = value * spread(ff[pl.ds(pl.multiple_of(k * 8, 8), 8), :], select_r)
        ur[k] = dot(map_t, scaled.astype(BF16))
        return 0

    def step_maps(k, _):
        at = pl.multiple_of(k * Q, Q)
        window = pb[pl.ds(at, Q + 2 * EDGE), Q:].astype(F32)
        cf = silu(taps(window, weights_s[:, Q:], [EDGE - 3, EDGE - 2, EDGE - 1, EDGE])).astype(BF16)
        gcf[pl.ds(at, Q), Q:] = cf
        gcf[pl.ds(at, Q), :Q] = jnp.where(r >= c, dot(cf, btf[pl.ds(at, Q), :]), 0.0).astype(BF16)
        cr = silu(taps(window, weights_s[:, Q:], [EDGE + 3, EDGE + 2, EDGE + 1, EDGE])).astype(BF16)
        gcr[pl.ds(at, Q), Q:] = cr
        gcr[pl.ds(at, Q), :Q] = jnp.where(r <= c, dot(cr, btr[pl.ds(at, Q), :]), 0.0).astype(BF16)
        return 0

    def step_reverse(k):
        at = pl.multiple_of(k * Q, Q)
        window = pm[pl.ds(EDGE + at, Q + EDGE), :].astype(F32)
        value = silu(taps(window, weights_x, [3, 2, 1, 0]))
        xr[pl.ds(at, Q), :] = value
        scaled = (value * spread(fr[pl.ds(pl.multiple_of(k * 8, 8), 8), :], select_f)).astype(BF16)
        xsr[k] = scaled
        ur[k] = dot(btr[pl.ds(at, Q), :], scaled)

    def step_forward(k, state):
        at = pl.multiple_of(k * Q, Q)
        window = pb[pl.ds(at, Q + EDGE), :Q].astype(F32)
        map_t = silu(taps(window, weights_s[:, :Q], [EDGE - 3, EDGE - 2, EDGE - 1, EDGE])).T.astype(BF16)
        btf[pl.ds(at, Q), :] = map_t
        window = px[pl.ds(at, Q + EDGE), :].astype(F32)
        value = silu(taps(window, weights_x, [EDGE - 3, EDGE - 2, EDGE - 1, EDGE]))
        xf[pl.ds(at, Q), :] = value
        scaled = (value * spread(ff[pl.ds(pl.multiple_of(k * 8, 8), 8), :], select_f)).astype(BF16)
        xsf[k] = scaled
        uf[k] = dot(map_t, scaled)
        return state

    def forward_total(k, state):
        e = exf[pl.ds(k, 1), :]
        return e * (e * state + uf[k])

    tot, got, inc = (tot_f, tot_r), (got_f, got_r), (inc_f, inc_r)

    def to_owner(way, d):
        peer = (here + d) & (seqs - 1)
        return pltpu.make_async_remote_copy(
            src_ref=tot[way].at[pl.ds(pl.multiple_of(peer * share, share), share)],
            dst_ref=got[way].at[here], send_sem=a_send.at[way], recv_sem=a_recv.at[way],
            device_id={"seq": peer, "head": mine}, device_id_type=MESH,
        )

    def from_owner(way, d):
        peer = (here + d) & (seqs - 1)
        landing = in_f.at[pl.ds(pl.multiple_of(here * share, share), share)] if way == 0 else in_r.at[here]
        return pltpu.make_async_remote_copy(
            src_ref=inc[way].at[peer], dst_ref=landing,
            send_sem=b_send.at[way], recv_sem=b_recv.at[way],
            device_id={"seq": peer, "head": mine if way == 0 else mate}, device_id_type=MESH,
        )

    mine_rows = pl.ds(pl.multiple_of(here * share, share), share)

    def others(buffer, sem, count=seqs - 1):
        span = buffer.at[pl.ds(0, count)]
        pltpu.make_async_copy(span, span, sem).wait()

    def states_out(way):
        def go(d, _):
            to_owner(way, d).start()
            return 0

        lax.fori_loop(1, seqs, go, 0)
        got[way][here] = tot[way][mine_rows, :]

    left = iota((1, Q), 1) < Q // 2

    def states_back(way):
        others(got[way], a_recv.at[way])

        def hop(i, entering):
            at = i if way == 0 else seqs - 1 - i
            if way == 0:
                inc_f[at] = entering
            else:
                inc_r[at] = jnp.concatenate([entering[:, :wing], entering[:, wing:]], axis=0).astype(BF16)
            d = [dall[at, HEADS * way + h : HEADS * way + h + 1, :] for h in range(HEADS)]
            decay = jnp.concatenate([jnp.where(left, d[0], d[1]), jnp.where(left, d[2], d[3])], axis=1)
            return decay * entering + got[way][at]

        lax.fori_loop(0, seqs, hop, jnp.zeros(got[way].shape[1:], F32))

        def go(d, _):
            from_owner(way, d).start()
            return 0

        lax.fori_loop(1 - way, seqs, go, 0)
        if way == 0:
            in_f[mine_rows, :] = inc_f[here]

    def entered():
        others(in_r, b_recv.at[1], seqs)
        blocks = [in_r[j].astype(F32) for j in range(seqs)]
        return jnp.concatenate([jnp.concatenate([b[:share], b[share:]], axis=1) for b in blocks], axis=0)

    each = chunks // PIECES

    def pieces(start, stop):
        def one(i, _):
            p = PIECES - 1 - i
            piece(p).wait_recv()

            for j in range(each):
                k = p * each + each - 1 - j
                step_reverse(k)
            return 0

        lax.fori_loop(start, stop, one, 0)

    def finish_forward(k, state, early):
        at = pl.multiple_of(k * Q, Q)
        e = exf[pl.ds(k, 1), :]
        entering = e * state
        y = dot(gcf[pl.ds(at, Q), :], jnp.concatenate([xsf[k], entering.astype(BF16)], axis=0))
        scale = spread(ef[pl.ds(pl.multiple_of(k * 8, 8), 8), :], select_f)
        y = scale * y + gain * xf[pl.ds(at, Q), :]
        if early:
            out_ref[pl.ds(at, Q), :] = (y + back[pl.ds(at, Q), :].astype(F32)).astype(BF16)
        else:
            yf[pl.ds(at, Q), :] = y
        return e * (entering + uf[k])

    def finish_reverse(k, state):
        at = pl.multiple_of(k * Q, Q)
        e = exr[pl.ds(k, 1), :]
        entering = e * state
        y = dot(gcr[pl.ds(at, Q), :], jnp.concatenate([xsr[k], entering.astype(BF16)], axis=0))
        scale = spread(er[pl.ds(pl.multiple_of(k * 8, 8), 8), :], select_f)
        return (scale * y + gain * xr[pl.ds(at, Q), :]).astype(BF16), e * (entering + ur[k])

    def finish_early(i, state):
        k = chunks - 1 - i
        back[pl.ds(pl.multiple_of(k * Q, Q), Q), :], state = finish_reverse(k, state)
        return state

    late = TAIL * each

    lax.fori_loop(0, chunks // 4 - 1, by(4, step_mate), 0)
    arrive_halos()
    lax.fori_loop(chunks // 4 - 1, chunks // 4, by(4, step_mate), 0)
    reverse_total()
    states_out(1)
    lax.fori_loop(0, chunks // 4, by(4, step_forward), 0)
    tot_f[...] = lax.fori_loop(0, chunks // 4, by(4, forward_total), jnp.zeros((Q, width), F32))
    states_out(0)
    lax.fori_loop(0, chunks // 4, by(4, step_maps), 0)
    half = steps_of(own8, mate * HEADS + local, 0, er, fr)
    exr[...] = chunk_decay(half, 0)
    everyone = dall.at[pl.ds(0, seqs - 1)]
    pltpu.make_async_copy(everyone, everyone, d_recv).wait()
    states_back(1)
    lax.fori_loop(6, PIECES, push, 0)
    halos[4].wait_recv()

    @pl.when(here == seqs - 1)
    def _():
        pm[pl.ds(rows + EDGE, EDGE), :] = jnp.zeros((EDGE, width), BF16)

    pieces(0, PIECES // 2)
    states_back(0)
    pieces(PIECES // 2, PIECES - TAIL)
    state = lax.fori_loop(0, (chunks - late) // 4, by(4, finish_early), entered())
    others(inc_f, b_recv.at[0])
    forward = lax.fori_loop(0, late // 4, by(4, lambda k, st: finish_forward(k, st, False)), in_f[...])
    lax.fori_loop(late // 4, chunks // 4, by(4, lambda k, st: finish_forward(k, st, True)), forward)

    def finish_late(i, state):
        p = TAIL - 1 - i
        piece(p).wait_recv()
        ks = [p * each + each - 1 - j for j in range(each)]
        for k in ks:
            step_reverse(k)
        for k in ks:
            at = pl.multiple_of(k * Q, Q)
            rounded, state = finish_reverse(k, state)
            out_ref[pl.ds(at, Q), :] = (yf[pl.ds(at, Q), :] + rounded.astype(F32)).astype(BF16)
        return state

    lax.fori_loop(0, TAIL, finish_late, state)

    for copy in halos:
        copy.wait_send()

    for p in range(PIECES):
        piece(p).wait_send()

    pltpu.make_async_copy(everyone, everyone, d_send).wait()
    for way in (0, 1):
        others(got[way], a_send.at[way])
        others(inc[way], b_send.at[way], seqs - 1 + way)


def per_device(inputs, bc_inputs, dt_raw, conv_inner, conv_state, log_rate, dt_bias, skip_gain):
    seqs, ways = lax.axis_size("seq"), lax.axis_size("head")
    rows, width = inputs.shape
    chunks, share, wing = rows // Q, Q // seqs, width // 2
    anywhere = pl.BlockSpec(memory_space=pl.ANY)
    vmem = pl.BlockSpec(memory_space=pltpu.VMEM)
    padded = pltpu.VMEM((rows + 2 * EDGE, width), BF16)
    steps, decays = pltpu.VMEM((chunks * 8, Q), F32), pltpu.VMEM((chunks, width), F32)
    dma = pltpu.SemaphoreType.DMA
    return pl.pallas_call(
        functools.partial(kernel, seqs, ways),
        out_shape=jax.ShapeDtypeStruct((rows, width), BF16),
        in_specs=[anywhere] * 8,
        out_specs=vmem,
        scratch_shapes=[
            pltpu.VMEM(conv_state.shape, F32), pltpu.VMEM((1, log_rate.shape[0]), F32),
            pltpu.VMEM((1, log_rate.shape[0]), F32), pltpu.VMEM((1, log_rate.shape[0]), F32),
            pltpu.VMEM(dt_raw.shape, BF16), pltpu.VMEM((4, width), F32), pltpu.VMEM((4, width), F32),
            padded, padded, padded,
            pltpu.VMEM((rows, 2 * Q), BF16), pltpu.VMEM((rows, 2 * Q), BF16),
            pltpu.VMEM((rows, Q), BF16), pltpu.VMEM((rows, Q), BF16),
            pltpu.VMEM((chunks, Q, width), BF16), pltpu.VMEM((chunks, Q, width), BF16),
            pltpu.VMEM((rows, width), F32), pltpu.VMEM((rows, width), F32),
            pltpu.VMEM((chunks, Q, width), F32), pltpu.VMEM((chunks, Q, width), F32),
            pltpu.VMEM((rows, width), F32),
            steps, steps, steps, steps, decays, decays, decays,
            pltpu.VMEM((rows, width), BF16), pltpu.VMEM((Q, width), F32), pltpu.VMEM((Q, width), F32),
            pltpu.VMEM((seqs, share, width), F32), pltpu.VMEM((seqs, share, width), F32),
            pltpu.VMEM((seqs, share, width), F32), pltpu.VMEM((seqs, 2 * share, wing), BF16),
            pltpu.VMEM((Q, width), F32), pltpu.VMEM((seqs, 2 * share, wing), BF16),
            pltpu.VMEM((8, Q), F32), pltpu.VMEM((seqs, 8, Q), F32),
            dma((9,)), dma((5,)), dma((5,)), dma((PIECES,)), dma((PIECES,)),
            dma, dma, dma((2,)), dma((2,)), dma((2,)), dma((2,)),
        ],
        compiler_params=pltpu.CompilerParams(
            collective_id=0, has_side_effects=True, vmem_limit_bytes=60 * 2**20
        ),
    )(
        inputs, bc_inputs, dt_raw, conv_inner, conv_state,
        log_rate[None, :], dt_bias[None, :], skip_gain[None, :],
    )


def solution(mesh):
    return jax.shard_map(
        per_device,
        mesh=mesh,
        in_specs=(P("seq", "head"), P("seq", None), P(None, "seq"), P(), P(), P(), P(), P()),
        out_specs=P("seq", "head"),
        check_vma=False,
    )
```

```python
import functools

import jax
import jax.numpy as jnp
from jax import lax
from jax.experimental import pallas as pl
from jax.experimental.pallas import tpu as pltpu
from jax.sharding import PartitionSpec as P

Q = 128
EDGE = 16
HEADS = 4
PIECES = 8
TAIL = 2
HIGHEST = lax.Precision.HIGHEST
MESH = pl.DeviceIdType.MESH
F32 = jnp.float32
BF16 = jnp.bfloat16


def iota(shape, dim):
    return lax.broadcasted_iota(jnp.int32, shape, dim)


def silu(v):
    h = 0.5 * v
    return h * jnp.tanh(h) + h


def taps(window, weights, begins):
    total = weights[0:1, :] * window[begins[0] : begins[0] + Q]
    for i in range(1, 4):
        total = total + weights[i : i + 1, :] * window[begins[i] : begins[i] + Q]
    return total


def dot(a, b):
    return jnp.dot(a, b, preferred_element_type=F32)


def dot_nt(a, b):
    return lax.dot_general(a, b, (((1,), (1,)), ((), ())), preferred_element_type=F32)


def spread(rows, select):
    high = rows.astype(BF16).astype(F32)
    parts = jnp.concatenate([high, rows - high], axis=0)
    return dot(parts.T.astype(BF16), select)


def kernel(
    seqs, ways,
    x_hbm, bc_hbm, dt_hbm, wx_hbm, ws_hbm, rate_hbm, bias_hbm, gain_hbm,
    out_ref,
    ws_ref, rate_ref, bias_ref, gain_ref, dt_ref, wx_ref, wm_ref, px, pb, pm, gcf, gcr, btr, btf, xsf, xsr, xf, xr, uf, ur, yf, ef, ff, er, fr, exf, exm, exr,
    back, tot_f, tot_r, got_f, got_r, inc_f, inc_r, in_f, in_r, dmsg, dall,
    local_sem, halo_send, halo_recv, piece_send, piece_recv,
    d_send, d_recv, a_send, a_recv, b_send, b_recv,
):
    rows, width = x_hbm.shape
    chunks = rows // Q
    share = Q // seqs
    wing = width // 2
    here, mine = lax.axis_index("seq"), lax.axis_index("head")
    mate = (mine + ways // 2) & (ways - 1)
    after, before = (here + 1) & (seqs - 1), (here - 1) & (seqs - 1)

    own_x = pltpu.make_async_copy(x_hbm, px.at[pl.ds(EDGE, rows)], local_sem.at[0])
    own_bc = pltpu.make_async_copy(bc_hbm, pb.at[pl.ds(EDGE, rows)], local_sem.at[1])
    own_dt = pltpu.make_async_copy(dt_hbm, dt_ref, local_sem.at[2])
    columns = pl.ds(pl.multiple_of(mine * width, width), width)
    theirs = pl.ds(pl.multiple_of(mate * width, width), width)
    mate_w = pltpu.make_async_copy(wx_hbm.at[:, theirs], wm_ref, local_sem.at[4])
    own_w = pltpu.make_async_copy(wx_hbm.at[:, columns], wx_ref, local_sem.at[3])

    barrier = pltpu.get_barrier_semaphore()

    def greet(d, _):
        peer = (here + d) & (seqs - 1)
        pl.semaphore_signal(barrier, inc=1, device_id={"seq": peer, "head": mine}, device_id_type=MESH)
        return 0

    def greet_mate(d, _):
        peer = (here + d) & (seqs - 1)
        pl.semaphore_signal(barrier, inc=1, device_id={"seq": peer, "head": mate}, device_id_type=MESH)
        return 0

    lax.fori_loop(1, seqs, greet, 0)
    lax.fori_loop(0, seqs, greet_mate, 0)
    small = [
        pltpu.make_async_copy(source, target, local_sem.at[5 + i])
        for i, (source, target) in enumerate(
            ((rate_hbm, rate_ref), (bias_hbm, bias_ref), (gain_hbm, gain_ref), (ws_hbm, ws_ref))
        )
    ]
    own_dt.start()
    for copy in small:
        copy.start()
    own_bc.start()
    own_x.start()
    own_w.start()
    mate_w.start()
    pl.semaphore_wait(barrier, 2 * seqs - 1)

    def halo(i, src, dst, s, h):
        return pltpu.make_async_remote_copy(
            src_ref=src, dst_ref=dst, send_sem=halo_send.at[i], recv_sem=halo_recv.at[i],
            device_id={"seq": s, "head": h}, device_id_type=MESH,
        )

    first, last = pl.ds(0, EDGE), pl.ds(rows - EDGE, EDGE)
    low, high = pl.ds(0, EDGE), pl.ds(rows + EDGE, EDGE)
    halos = [
        halo(0, bc_hbm.at[last], pb.at[low], after, mine),
        halo(1, bc_hbm.at[first], pb.at[high], before, mine),
        halo(2, x_hbm.at[last], px.at[low], after, mine),
        halo(3, x_hbm.at[first], px.at[high], before, mine),
        halo(4, x_hbm.at[first], pm.at[high], before, mate),
    ]
    for copy in halos:
        copy.start()
    length = rows // PIECES

    def piece(p):
        at = pl.multiple_of(p * length, length)
        return pltpu.make_async_remote_copy(
            src_ref=x_hbm.at[pl.ds(at, length)], dst_ref=pm.at[pl.ds(EDGE + at, length)],
            send_sem=piece_send.at[p], recv_sem=piece_recv.at[p],
            device_id={"seq": here, "head": mate}, device_id_type=MESH,
        )

    def push(i, _):
        piece(PIECES - 1 - i).start()
        return 0

    lax.fori_loop(0, 6, push, 0)

    own_dt.wait()
    for copy in small:
        copy.wait()

    all_heads = dt_ref.shape[0]
    row8, head8 = iota((8, all_heads), 0), iota((8, all_heads), 1)
    r, c = iota((Q, Q), 0), iota((Q, Q), 1)
    per = width // HEADS
    head_row, head_col = iota((chunks * 8, width), 0) & 7, iota((chunks * 8, width), 1) // per
    to_chunk = (iota((chunks, chunks * 8), 1) // 8 == iota((chunks, chunks * 8), 0)).astype(F32)

    def pick(owner8, values):
        return jnp.sum(jnp.where(head8 == owner8, values, 0.0), axis=1, keepdims=True)

    def stack(values):
        return jnp.concatenate([values[:, k * Q : (k + 1) * Q] for k in range(chunks)], axis=0)

    def steps_of(owner8, source8, forwards, e_ref, f_ref):
        raw8 = dot((head8 == source8).astype(F32).astype(BF16), dt_ref[...])
        rate8 = pick(owner8, -jnp.exp(rate_ref[...]))
        pre = raw8 + pick(owner8, bias_ref[...])
        dt8 = jnp.maximum(pre, 0.0) + jnp.log1p(jnp.exp(-jnp.abs(pre)))
        logs = stack(dt8 * rate8)
        cum = jnp.dot(logs, (r >= c).astype(F32), precision=HIGHEST, preferred_element_type=F32)
        if forwards:
            upto = jnp.dot(logs, (r <= c).astype(F32), precision=HIGHEST, preferred_element_type=F32)
            cum = jnp.where((iota((chunks * 8, Q), 0) & 7) < forwards, upto, cum)
        half = 0.5 * jnp.sum(logs, axis=1, keepdims=True)
        e_ref[...] = jnp.exp(cum - half)
        f_ref[...] = stack(dt8) * jnp.exp(half - cum)
        return half

    def chunk_decay(half, offset):
        wide = jnp.where(head_row == head_col + offset, half, 0.0)
        return jnp.exp(jnp.dot(to_chunk, wide, precision=HIGHEST, preferred_element_type=F32))

    local = row8 & (HEADS - 1)
    own8 = mine * HEADS + local
    half = steps_of(jnp.where(row8 < HEADS, mine, mate) * HEADS + local, own8, HEADS, ef, ff)
    exf[...] = chunk_decay(half, 0)
    exm[...] = chunk_decay(half, HEADS)
    gain = jnp.sum(
        jnp.where(iota((8, width), 0) == iota((8, width), 1) // per, pick(own8, gain_ref[...]), 0.0),
        axis=0, keepdims=True,
    )
    sel_row, sel_col = iota((16, width), 0) & 7, iota((16, width), 1) // per
    select_f = (sel_row == sel_col).astype(F32).astype(BF16)
    select_r = (sel_row == sel_col + HEADS).astype(F32).astype(BF16)
    all_logs = sum(half[8 * k : 8 * k + 8, :] for k in range(chunks))
    decay = jnp.broadcast_to(jnp.exp(2.0 * all_logs), (8, Q))
    dmsg[...] = decay
    dall[here] = decay

    def tell(d):
        return pltpu.make_async_remote_copy(
            src_ref=dmsg, dst_ref=dall.at[here], send_sem=d_send, recv_sem=d_recv,
            device_id={"seq": (here + d) & (seqs - 1), "head": mine}, device_id_type=MESH,
        )

    def tell_start(d, _):
        tell(d).start()
        return 0

    lax.fori_loop(1, seqs, tell_start, 0)

    own_w.wait()
    mate_w.wait()
    weights_x = wx_ref[...]
    weights_m = wm_ref[...]
    weights_s = ws_ref[...]

    own_x.wait()
    own_bc.wait()
    def by(n, body):
        def several(i, state):
            for j in range(n):
                state = body(n * i + j, state)
            return state

        return several

    def arrive_halos():
        for i in range(4):
            halos[i].wait_recv()

        @pl.when(here == 0)
        def _():
            px[pl.ds(0, EDGE), :] = jnp.zeros((EDGE, width), BF16)
            pb[pl.ds(0, EDGE), :] = jnp.zeros((EDGE, width), BF16)

        @pl.when(here == seqs - 1)
        def _():
            pb[pl.ds(rows + EDGE, EDGE), :] = jnp.zeros((EDGE, width), BF16)
            px[pl.ds(rows + EDGE, EDGE), :] = jnp.zeros((EDGE, width), BF16)

    def reverse_total():
        def step(i, state):
            k = chunks - 1 - i
            e = exm[pl.ds(k, 1), :]
            return e * (e * state + ur[k])

        tot_r[...] = lax.fori_loop(0, chunks // 4, by(4, step), jnp.zeros((Q, width), F32))

    def step_mate(k, _):
        at = pl.multiple_of(k * Q, Q)
        window = pb[pl.ds(EDGE + at, Q + EDGE), :Q].astype(F32)
        map_t = silu(taps(window, weights_s[:, :Q], [3, 2, 1, 0])).T.astype(BF16)
        btr[pl.ds(at, Q), :] = map_t
        window = px[pl.ds(EDGE + at, Q + EDGE), :].astype(F32)
        value = silu(taps(window, weights_m, [3, 2, 1, 0]))
        scaled = value * spread(ff[pl.ds(pl.multiple_of(k * 8, 8), 8), :], select_r)
        ur[k] = dot(map_t, scaled.astype(BF16))
        return 0

    def step_maps(k, _):
        at = pl.multiple_of(k * Q, Q)
        window = pb[pl.ds(at, Q + 2 * EDGE), Q:].astype(F32)
        cf = silu(taps(window, weights_s[:, Q:], [EDGE - 3, EDGE - 2, EDGE - 1, EDGE])).astype(BF16)
        gcf[pl.ds(at, Q), Q:] = cf
        gcf[pl.ds(at, Q), :Q] = jnp.where(r >= c, dot(cf, btf[pl.ds(at, Q), :]), 0.0).astype(BF16)
        cr = silu(taps(window, weights_s[:, Q:], [EDGE + 3, EDGE + 2, EDGE + 1, EDGE])).astype(BF16)
        gcr[pl.ds(at, Q), Q:] = cr
        gcr[pl.ds(at, Q), :Q] = jnp.where(r <= c, dot(cr, btr[pl.ds(at, Q), :]), 0.0).astype(BF16)
        return 0

    def step_reverse(k):
        at = pl.multiple_of(k * Q, Q)
        window = pm[pl.ds(EDGE + at, Q + EDGE), :].astype(F32)
        value = silu(taps(window, weights_x, [3, 2, 1, 0]))
        xr[pl.ds(at, Q), :] = value
        scaled = (value * spread(fr[pl.ds(pl.multiple_of(k * 8, 8), 8), :], select_f)).astype(BF16)
        xsr[k] = scaled
        ur[k] = dot(btr[pl.ds(at, Q), :], scaled)

    def step_forward(k, state):
        at = pl.multiple_of(k * Q, Q)
        window = pb[pl.ds(at, Q + EDGE), :Q].astype(F32)
        map_t = silu(taps(window, weights_s[:, :Q], [EDGE - 3, EDGE - 2, EDGE - 1, EDGE])).T.astype(BF16)
        btf[pl.ds(at, Q), :] = map_t
        window = px[pl.ds(at, Q + EDGE), :].astype(F32)
        value = silu(taps(window, weights_x, [EDGE - 3, EDGE - 2, EDGE - 1, EDGE]))
        xf[pl.ds(at, Q), :] = value
        scaled = (value * spread(ff[pl.ds(pl.multiple_of(k * 8, 8), 8), :], select_f)).astype(BF16)
        xsf[k] = scaled
        uf[k] = dot(map_t, scaled)
        return state

    def forward_total(k, state):
        e = exf[pl.ds(k, 1), :]
        return e * (e * state + uf[k])

    tot, got, inc = (tot_f, tot_r), (got_f, got_r), (inc_f, inc_r)

    def to_owner(way, d):
        peer = (here + d) & (seqs - 1)
        return pltpu.make_async_remote_copy(
            src_ref=tot[way].at[pl.ds(pl.multiple_of(peer * share, share), share)],
            dst_ref=got[way].at[here], send_sem=a_send.at[way], recv_sem=a_recv.at[way],
            device_id={"seq": peer, "head": mine}, device_id_type=MESH,
        )

    def from_owner(way, d):
        peer = (here + d) & (seqs - 1)
        landing = in_f.at[pl.ds(pl.multiple_of(here * share, share), share)] if way == 0 else in_r.at[here]
        return pltpu.make_async_remote_copy(
            src_ref=inc[way].at[peer], dst_ref=landing,
            send_sem=b_send.at[way], recv_sem=b_recv.at[way],
            device_id={"seq": peer, "head": mine if way == 0 else mate}, device_id_type=MESH,
        )

    mine_rows = pl.ds(pl.multiple_of(here * share, share), share)

    def others(buffer, sem, count=seqs - 1):
        span = buffer.at[pl.ds(0, count)]
        pltpu.make_async_copy(span, span, sem).wait()

    def far_first(d):
        moved = d + seqs // 4 - 1
        moved = jnp.where(moved > seqs - 1, moved - (seqs - 1), moved)
        return jnp.where(d == 0, 0, moved)

    def states_out(way):
        def go(d, _):
            to_owner(way, far_first(d)).start()
            return 0

        lax.fori_loop(1, seqs, go, 0)
        got[way][here] = tot[way][mine_rows, :]

    left = iota((1, Q), 1) < Q // 2

    def states_back(way):
        others(got[way], a_recv.at[way])

        def hop(i, entering):
            at = i if way == 0 else seqs - 1 - i
            if way == 0:
                inc_f[at] = entering
            else:
                inc_r[at] = jnp.concatenate([entering[:, :wing], entering[:, wing:]], axis=0).astype(BF16)
            d = [dall[at, HEADS * way + h : HEADS * way + h + 1, :] for h in range(HEADS)]
            decay = jnp.concatenate([jnp.where(left, d[0], d[1]), jnp.where(left, d[2], d[3])], axis=1)
            return decay * entering + got[way][at]

        lax.fori_loop(0, seqs, hop, jnp.zeros(got[way].shape[1:], F32))

        def go(d, _):
            from_owner(way, far_first(d)).start()
            return 0

        lax.fori_loop(1 - way, seqs, go, 0)
        if way == 0:
            in_f[mine_rows, :] = inc_f[here]

    def entered():
        others(in_r, b_recv.at[1], seqs)
        blocks = [in_r[j].astype(F32) for j in range(seqs)]
        return jnp.concatenate([jnp.concatenate([b[:share], b[share:]], axis=1) for b in blocks], axis=0)

    each = chunks // PIECES

    def pieces(start, stop):
        def one(i, _):
            p = PIECES - 1 - i
            piece(p).wait_recv()

            for j in range(each):
                k = p * each + each - 1 - j
                step_reverse(k)
            return 0

        lax.fori_loop(start, stop, one, 0)

    def finish_forward(k, state, early):
        at = pl.multiple_of(k * Q, Q)
        e = exf[pl.ds(k, 1), :]
        entering = e * state
        y = dot(gcf[pl.ds(at, Q), :], jnp.concatenate([xsf[k], entering.astype(BF16)], axis=0))
        scale = spread(ef[pl.ds(pl.multiple_of(k * 8, 8), 8), :], select_f)
        y = scale * y + gain * xf[pl.ds(at, Q), :]
        if early:
            out_ref[pl.ds(at, Q), :] = (y + back[pl.ds(at, Q), :].astype(F32)).astype(BF16)
        else:
            yf[pl.ds(at, Q), :] = y
        return e * (entering + uf[k])

    def finish_reverse(k, state):
        at = pl.multiple_of(k * Q, Q)
        e = exr[pl.ds(k, 1), :]
        entering = e * state
        y = dot(gcr[pl.ds(at, Q), :], jnp.concatenate([xsr[k], entering.astype(BF16)], axis=0))
        scale = spread(er[pl.ds(pl.multiple_of(k * 8, 8), 8), :], select_f)
        return (scale * y + gain * xr[pl.ds(at, Q), :]).astype(BF16), e * (entering + ur[k])

    def finish_early(i, state):
        k = chunks - 1 - i
        back[pl.ds(pl.multiple_of(k * Q, Q), Q), :], state = finish_reverse(k, state)
        return state

    late = TAIL * each

    lax.fori_loop(0, chunks // 4 - 1, by(4, step_mate), 0)
    arrive_halos()
    lax.fori_loop(chunks // 4 - 1, chunks // 4, by(4, step_mate), 0)
    reverse_total()
    states_out(1)
    lax.fori_loop(0, chunks // 4, by(4, step_forward), 0)
    tot_f[...] = lax.fori_loop(0, chunks // 4, by(4, forward_total), jnp.zeros((Q, width), F32))
    states_out(0)
    lax.fori_loop(0, chunks // 4, by(4, step_maps), 0)
    everyone = dall.at[pl.ds(0, seqs - 1)]
    pltpu.make_async_copy(everyone, everyone, d_recv).wait()
    states_back(1)
    lax.fori_loop(6, PIECES, push, 0)
    half = steps_of(own8, mate * HEADS + local, 0, er, fr)
    exr[...] = chunk_decay(half, 0)
    halos[4].wait_recv()

    @pl.when(here == seqs - 1)
    def _():
        pm[pl.ds(rows + EDGE, EDGE), :] = jnp.zeros((EDGE, width), BF16)

    pieces(0, PIECES // 2)
    states_back(0)
    pieces(PIECES // 2, PIECES - TAIL)
    state = lax.fori_loop(0, (chunks - late) // 4, by(4, finish_early), entered())
    others(inc_f, b_recv.at[0])
    forward = lax.fori_loop(0, late // 4, by(4, lambda k, st: finish_forward(k, st, False)), in_f[...])
    lax.fori_loop(late // 4, chunks // 4, by(4, lambda k, st: finish_forward(k, st, True)), forward)

    def finish_late(i, state):
        p = TAIL - 1 - i
        piece(p).wait_recv()
        ks = [p * each + each - 1 - j for j in range(each)]
        for k in ks:
            step_reverse(k)
        for k in ks:
            at = pl.multiple_of(k * Q, Q)
            rounded, state = finish_reverse(k, state)
            out_ref[pl.ds(at, Q), :] = (yf[pl.ds(at, Q), :] + rounded.astype(F32)).astype(BF16)
        return state

    lax.fori_loop(0, TAIL, finish_late, state)

    for copy in halos:
        copy.wait_send()

    for p in range(PIECES):
        piece(p).wait_send()

    pltpu.make_async_copy(everyone, everyone, d_send).wait()
    for way in (0, 1):
        others(got[way], a_send.at[way])
        others(inc[way], b_send.at[way], seqs - 1 + way)


def per_device(inputs, bc_inputs, dt_raw, conv_inner, conv_state, log_rate, dt_bias, skip_gain):
    seqs, ways = lax.axis_size("seq"), lax.axis_size("head")
    rows, width = inputs.shape
    chunks, share, wing = rows // Q, Q // seqs, width // 2
    anywhere = pl.BlockSpec(memory_space=pl.ANY)
    vmem = pl.BlockSpec(memory_space=pltpu.VMEM)
    padded = pltpu.VMEM((rows + 2 * EDGE, width), BF16)
    steps, decays = pltpu.VMEM((chunks * 8, Q), F32), pltpu.VMEM((chunks, width), F32)
    dma = pltpu.SemaphoreType.DMA
    return pl.pallas_call(
        functools.partial(kernel, seqs, ways),
        out_shape=jax.ShapeDtypeStruct((rows, width), BF16),
        in_specs=[anywhere] * 8,
        out_specs=vmem,
        scratch_shapes=[
            pltpu.VMEM(conv_state.shape, F32), pltpu.VMEM((1, log_rate.shape[0]), F32),
            pltpu.VMEM((1, log_rate.shape[0]), F32), pltpu.VMEM((1, log_rate.shape[0]), F32),
            pltpu.VMEM(dt_raw.shape, BF16), pltpu.VMEM((4, width), F32), pltpu.VMEM((4, width), F32),
            padded, padded, padded,
            pltpu.VMEM((rows, 2 * Q), BF16), pltpu.VMEM((rows, 2 * Q), BF16),
            pltpu.VMEM((rows, Q), BF16), pltpu.VMEM((rows, Q), BF16),
            pltpu.VMEM((chunks, Q, width), BF16), pltpu.VMEM((chunks, Q, width), BF16),
            pltpu.VMEM((rows, width), F32), pltpu.VMEM((rows, width), F32),
            pltpu.VMEM((chunks, Q, width), F32), pltpu.VMEM((chunks, Q, width), F32),
            pltpu.VMEM((rows, width), F32),
            steps, steps, steps, steps, decays, decays, decays,
            pltpu.VMEM((rows, width), BF16), pltpu.VMEM((Q, width), F32), pltpu.VMEM((Q, width), F32),
            pltpu.VMEM((seqs, share, width), F32), pltpu.VMEM((seqs, share, width), F32),
            pltpu.VMEM((seqs, share, width), F32), pltpu.VMEM((seqs, 2 * share, wing), BF16),
            pltpu.VMEM((Q, width), F32), pltpu.VMEM((seqs, 2 * share, wing), BF16),
            pltpu.VMEM((8, Q), F32), pltpu.VMEM((seqs, 8, Q), F32),
            dma((9,)), dma((5,)), dma((5,)), dma((PIECES,)), dma((PIECES,)),
            dma, dma, dma((2,)), dma((2,)), dma((2,)), dma((2,)),
        ],
        compiler_params=pltpu.CompilerParams(
            collective_id=0, has_side_effects=True, vmem_limit_bytes=60 * 2**20
        ),
    )(
        inputs, bc_inputs, dt_raw, conv_inner, conv_state,
        log_rate[None, :], dt_bias[None, :], skip_gain[None, :],
    )


def solution(mesh):
    return jax.shard_map(
        per_device,
        mesh=mesh,
        in_specs=(P("seq", "head"), P("seq", None), P(None, "seq"), P(), P(), P(), P(), P()),
        out_specs=P("seq", "head"),
        check_vma=False,
    )
```

```python
import functools

import jax
import jax.numpy as jnp
from jax import lax
from jax.experimental import pallas as pl
from jax.experimental.pallas import tpu as pltpu
from jax.sharding import PartitionSpec as P

Q = 128
EDGE = 16
HEADS = 4
PIECES = 8
TAIL = 2
HIGHEST = lax.Precision.HIGHEST
MESH = pl.DeviceIdType.MESH
F32 = jnp.float32
BF16 = jnp.bfloat16


def iota(shape, dim):
    return lax.broadcasted_iota(jnp.int32, shape, dim)


def silu(v):
    h = 0.5 * v
    return h * jnp.tanh(h) + h


def taps(window, weights, begins):
    total = weights[0:1, :] * window[begins[0] : begins[0] + Q]
    for i in range(1, 4):
        total = total + weights[i : i + 1, :] * window[begins[i] : begins[i] + Q]
    return total


def dot(a, b):
    return jnp.dot(a, b, preferred_element_type=F32)


def dot_nt(a, b):
    return lax.dot_general(a, b, (((1,), (1,)), ((), ())), preferred_element_type=F32)


def spread(rows, select):
    high = rows.astype(BF16).astype(F32)
    parts = jnp.concatenate([high, rows - high], axis=0)
    return dot(parts.T.astype(BF16), select)


def kernel(
    seqs, ways,
    x_hbm, bc_hbm, dt_hbm, wx_hbm, ws_hbm, rate_hbm, bias_hbm, gain_hbm,
    out_ref,
    ws_ref, rate_ref, bias_ref, gain_ref, dt_ref, wx_ref, wm_ref, px, pb, pm, gcf, gcr, btr, btf, xsf, xsr, xf, xr, uf, ur, yf, ef, ff, er, fr, exf, exm, exr,
    back, tot_f, tot_r, got_f, got_r, inc_f, inc_r, in_f, in_r, dmsg, dall,
    local_sem, halo_send, halo_recv, piece_send, piece_recv,
    d_send, d_recv, a_send, a_recv, b_send, b_recv,
):
    rows, width = x_hbm.shape
    chunks = rows // Q
    share = Q // seqs
    wing = width // 2
    here, mine = lax.axis_index("seq"), lax.axis_index("head")
    mate = (mine + ways // 2) & (ways - 1)
    after, before = (here + 1) & (seqs - 1), (here - 1) & (seqs - 1)

    own_x = pltpu.make_async_copy(x_hbm, px.at[pl.ds(EDGE, rows)], local_sem.at[0])
    own_bc = pltpu.make_async_copy(bc_hbm, pb.at[pl.ds(EDGE, rows)], local_sem.at[1])
    own_dt = pltpu.make_async_copy(dt_hbm, dt_ref, local_sem.at[2])
    columns = pl.ds(pl.multiple_of(mine * width, width), width)
    theirs = pl.ds(pl.multiple_of(mate * width, width), width)
    mate_w = pltpu.make_async_copy(wx_hbm.at[:, theirs], wm_ref, local_sem.at[4])
    own_w = pltpu.make_async_copy(wx_hbm.at[:, columns], wx_ref, local_sem.at[3])

    barrier = pltpu.get_barrier_semaphore()

    def greet(d, _):
        peer = (here + d) & (seqs - 1)
        pl.semaphore_signal(barrier, inc=1, device_id={"seq": peer, "head": mine}, device_id_type=MESH)
        return 0

    def greet_mate(d, _):
        peer = (here + d) & (seqs - 1)
        pl.semaphore_signal(barrier, inc=1, device_id={"seq": peer, "head": mate}, device_id_type=MESH)
        return 0

    lax.fori_loop(1, seqs, greet, 0)
    lax.fori_loop(0, seqs, greet_mate, 0)
    small = [
        pltpu.make_async_copy(source, target, local_sem.at[5 + i])
        for i, (source, target) in enumerate(
            ((rate_hbm, rate_ref), (bias_hbm, bias_ref), (gain_hbm, gain_ref), (ws_hbm, ws_ref))
        )
    ]
    own_dt.start()
    for copy in small:
        copy.start()
    own_bc.start()
    own_x.start()
    own_w.start()
    mate_w.start()
    pl.semaphore_wait(barrier, 2 * seqs - 1)

    def halo(i, src, dst, s, h):
        return pltpu.make_async_remote_copy(
            src_ref=src, dst_ref=dst, send_sem=halo_send.at[i], recv_sem=halo_recv.at[i],
            device_id={"seq": s, "head": h}, device_id_type=MESH,
        )

    first, last = pl.ds(0, EDGE), pl.ds(rows - EDGE, EDGE)
    low, high = pl.ds(0, EDGE), pl.ds(rows + EDGE, EDGE)
    halos = [
        halo(0, bc_hbm.at[last], pb.at[low], after, mine),
        halo(1, bc_hbm.at[first], pb.at[high], before, mine),
        halo(2, x_hbm.at[last], px.at[low], after, mine),
        halo(3, x_hbm.at[first], px.at[high], before, mine),
        halo(4, x_hbm.at[first], pm.at[high], before, mate),
    ]
    for copy in halos:
        copy.start()
    length = rows // PIECES

    def piece(p):
        at = pl.multiple_of(p * length, length)
        return pltpu.make_async_remote_copy(
            src_ref=x_hbm.at[pl.ds(at, length)], dst_ref=pm.at[pl.ds(EDGE + at, length)],
            send_sem=piece_send.at[p], recv_sem=piece_recv.at[p],
            device_id={"seq": here, "head": mate}, device_id_type=MESH,
        )

    def push(i, _):
        piece(PIECES - 1 - i).start()
        return 0

    lax.fori_loop(0, 6, push, 0)

    own_dt.wait()
    for copy in small:
        copy.wait()

    all_heads = dt_ref.shape[0]
    row8, head8 = iota((8, all_heads), 0), iota((8, all_heads), 1)
    r, c = iota((Q, Q), 0), iota((Q, Q), 1)
    per = width // HEADS
    head_row, head_col = iota((chunks * 8, width), 0) & 7, iota((chunks * 8, width), 1) // per
    to_chunk = (iota((chunks, chunks * 8), 1) // 8 == iota((chunks, chunks * 8), 0)).astype(F32)

    def pick(owner8, values):
        return jnp.sum(jnp.where(head8 == owner8, values, 0.0), axis=1, keepdims=True)

    def stack(values):
        return jnp.concatenate([values[:, k * Q : (k + 1) * Q] for k in range(chunks)], axis=0)

    def steps_of(owner8, source8, forwards, e_ref, f_ref):
        raw8 = dot((head8 == source8).astype(F32).astype(BF16), dt_ref[...])
        rate8 = pick(owner8, -jnp.exp(rate_ref[...]))
        pre = raw8 + pick(owner8, bias_ref[...])
        dt8 = jnp.maximum(pre, 0.0) + jnp.log1p(jnp.exp(-jnp.abs(pre)))
        logs = stack(dt8 * rate8)
        cum = jnp.dot(logs, (r >= c).astype(F32), precision=HIGHEST, preferred_element_type=F32)
        if forwards:
            upto = jnp.dot(logs, (r <= c).astype(F32), precision=HIGHEST, preferred_element_type=F32)
            cum = jnp.where((iota((chunks * 8, Q), 0) & 7) < forwards, upto, cum)
        half = 0.5 * jnp.sum(logs, axis=1, keepdims=True)
        e_ref[...] = jnp.exp(cum - half)
        f_ref[...] = stack(dt8) * jnp.exp(half - cum)
        return half

    def chunk_decay(half, offset):
        wide = jnp.where(head_row == head_col + offset, half, 0.0)
        return jnp.exp(jnp.dot(to_chunk, wide, precision=HIGHEST, preferred_element_type=F32))

    local = row8 & (HEADS - 1)
    own8 = mine * HEADS + local
    half = steps_of(jnp.where(row8 < HEADS, mine, mate) * HEADS + local, own8, HEADS, ef, ff)
    exf[...] = chunk_decay(half, 0)
    exm[...] = chunk_decay(half, HEADS)
    gain = jnp.sum(
        jnp.where(iota((8, width), 0) == iota((8, width), 1) // per, pick(own8, gain_ref[...]), 0.0),
        axis=0, keepdims=True,
    )
    sel_row, sel_col = iota((16, width), 0) & 7, iota((16, width), 1) // per
    select_f = (sel_row == sel_col).astype(F32).astype(BF16)
    select_r = (sel_row == sel_col + HEADS).astype(F32).astype(BF16)
    all_logs = sum(half[8 * k : 8 * k + 8, :] for k in range(chunks))
    decay = jnp.broadcast_to(jnp.exp(2.0 * all_logs), (8, Q))
    dmsg[...] = decay
    dall[here] = decay

    def tell(d):
        return pltpu.make_async_remote_copy(
            src_ref=dmsg, dst_ref=dall.at[here], send_sem=d_send, recv_sem=d_recv,
            device_id={"seq": (here + d) & (seqs - 1), "head": mine}, device_id_type=MESH,
        )

    def tell_start(d, _):
        tell(d).start()
        return 0

    lax.fori_loop(1, seqs, tell_start, 0)

    own_w.wait()
    mate_w.wait()
    weights_x = wx_ref[...]
    weights_m = wm_ref[...]
    weights_s = ws_ref[...]

    own_x.wait()
    own_bc.wait()
    def by(n, body):
        def several(i, state):
            for j in range(n):
                state = body(n * i + j, state)
            return state

        return several

    def arrive_halos():
        for i in range(4):
            halos[i].wait_recv()

        @pl.when(here == 0)
        def _():
            px[pl.ds(0, EDGE), :] = jnp.zeros((EDGE, width), BF16)
            pb[pl.ds(0, EDGE), :] = jnp.zeros((EDGE, width), BF16)

        @pl.when(here == seqs - 1)
        def _():
            pb[pl.ds(rows + EDGE, EDGE), :] = jnp.zeros((EDGE, width), BF16)
            px[pl.ds(rows + EDGE, EDGE), :] = jnp.zeros((EDGE, width), BF16)

    def reverse_total():
        def step(i, state):
            k = chunks - 1 - i
            e = exm[pl.ds(k, 1), :]
            return e * (e * state + ur[k])

        tot_r[...] = lax.fori_loop(0, chunks // 4, by(4, step), jnp.zeros((Q, width), F32))

    def step_mate(k, _):
        at = pl.multiple_of(k * Q, Q)
        window = pb[pl.ds(EDGE + at, Q + EDGE), :Q].astype(F32)
        map_t = silu(taps(window, weights_s[:, :Q], [3, 2, 1, 0])).T.astype(BF16)
        btr[pl.ds(at, Q), :] = map_t
        window = px[pl.ds(EDGE + at, Q + EDGE), :].astype(F32)
        value = silu(taps(window, weights_m, [3, 2, 1, 0]))
        scaled = value * spread(ff[pl.ds(pl.multiple_of(k * 8, 8), 8), :], select_r)
        ur[k] = dot(map_t, scaled.astype(BF16))
        return 0

    def step_maps(k, _):
        at = pl.multiple_of(k * Q, Q)
        window = pb[pl.ds(at, Q + 2 * EDGE), Q:].astype(F32)
        cf = silu(taps(window, weights_s[:, Q:], [EDGE - 3, EDGE - 2, EDGE - 1, EDGE])).astype(BF16)
        gcf[pl.ds(at, Q), Q:] = cf
        gcf[pl.ds(at, Q), :Q] = jnp.where(r >= c, dot(cf, btf[pl.ds(at, Q), :]), 0.0).astype(BF16)
        cr = silu(taps(window, weights_s[:, Q:], [EDGE + 3, EDGE + 2, EDGE + 1, EDGE])).astype(BF16)
        gcr[pl.ds(at, Q), Q:] = cr
        gcr[pl.ds(at, Q), :Q] = jnp.where(r <= c, dot(cr, btr[pl.ds(at, Q), :]), 0.0).astype(BF16)
        return 0

    def step_reverse(k):
        at = pl.multiple_of(k * Q, Q)
        window = pm[pl.ds(EDGE + at, Q + EDGE), :].astype(F32)
        value = silu(taps(window, weights_x, [3, 2, 1, 0]))
        xr[pl.ds(at, Q), :] = value
        scaled = (value * spread(fr[pl.ds(pl.multiple_of(k * 8, 8), 8), :], select_f)).astype(BF16)
        xsr[k] = scaled
        ur[k] = dot(btr[pl.ds(at, Q), :], scaled)

    def step_forward(k, state):
        at = pl.multiple_of(k * Q, Q)
        window = pb[pl.ds(at, Q + EDGE), :Q].astype(F32)
        map_t = silu(taps(window, weights_s[:, :Q], [EDGE - 3, EDGE - 2, EDGE - 1, EDGE])).T.astype(BF16)
        btf[pl.ds(at, Q), :] = map_t
        window = px[pl.ds(at, Q + EDGE), :].astype(F32)
        value = silu(taps(window, weights_x, [EDGE - 3, EDGE - 2, EDGE - 1, EDGE]))
        xf[pl.ds(at, Q), :] = value
        scaled = (value * spread(ff[pl.ds(pl.multiple_of(k * 8, 8), 8), :], select_f)).astype(BF16)
        xsf[k] = scaled
        uf[k] = dot(map_t, scaled)
        return state

    def forward_total(k, state):
        e = exf[pl.ds(k, 1), :]
        return e * (e * state + uf[k])

    tot, got, inc = (tot_f, tot_r), (got_f, got_r), (inc_f, inc_r)

    def to_owner(way, d):
        peer = (here + d) & (seqs - 1)
        return pltpu.make_async_remote_copy(
            src_ref=tot[way].at[pl.ds(pl.multiple_of(peer * share, share), share)],
            dst_ref=got[way].at[here], send_sem=a_send.at[way], recv_sem=a_recv.at[way],
            device_id={"seq": peer, "head": mine}, device_id_type=MESH,
        )

    def from_owner(way, d):
        peer = (here + d) & (seqs - 1)
        landing = in_f.at[pl.ds(pl.multiple_of(here * share, share), share)] if way == 0 else in_r.at[here]
        return pltpu.make_async_remote_copy(
            src_ref=inc[way].at[peer], dst_ref=landing,
            send_sem=b_send.at[way], recv_sem=b_recv.at[way],
            device_id={"seq": peer, "head": mine if way == 0 else mate}, device_id_type=MESH,
        )

    mine_rows = pl.ds(pl.multiple_of(here * share, share), share)

    def others(buffer, sem, count=seqs - 1):
        span = buffer.at[pl.ds(0, count)]
        pltpu.make_async_copy(span, span, sem).wait()

    def states_out(way):
        def go(d, _):
            to_owner(way, d).start()
            return 0

        lax.fori_loop(1, seqs, go, 0)
        got[way][here] = tot[way][mine_rows, :]

    left = iota((1, Q), 1) < Q // 2

    def states_back(way):
        others(got[way], a_recv.at[way])

        def hop(i, entering):
            at = i if way == 0 else seqs - 1 - i
            if way == 0:
                inc_f[at] = entering
            else:
                inc_r[at] = jnp.concatenate([entering[:, :wing], entering[:, wing:]], axis=0).astype(BF16)
            d = [dall[at, HEADS * way + h : HEADS * way + h + 1, :] for h in range(HEADS)]
            decay = jnp.concatenate([jnp.where(left, d[0], d[1]), jnp.where(left, d[2], d[3])], axis=1)
            return decay * entering + got[way][at]

        lax.fori_loop(0, seqs, hop, jnp.zeros(got[way].shape[1:], F32))

        def go(d, _):
            from_owner(way, d).start()
            return 0

        lax.fori_loop(1 - way, seqs, go, 0)
        if way == 0:
            in_f[mine_rows, :] = inc_f[here]

    def entered():
        others(in_r, b_recv.at[1], seqs)
        blocks = [in_r[j].astype(F32) for j in range(seqs)]
        return jnp.concatenate([jnp.concatenate([b[:share], b[share:]], axis=1) for b in blocks], axis=0)

    each = chunks // PIECES

    def pieces(start, stop):
        def one(i, _):
            p = PIECES - 1 - i
            piece(p).wait_recv()

            for j in range(each):
                k = p * each + each - 1 - j
                step_reverse(k)
            return 0

        lax.fori_loop(start, stop, one, 0)

    def finish_forward(k, state, early):
        at = pl.multiple_of(k * Q, Q)
        e = exf[pl.ds(k, 1), :]
        entering = e * state
        y = dot(gcf[pl.ds(at, Q), :], jnp.concatenate([xsf[k], entering.astype(BF16)], axis=0))
        scale = spread(ef[pl.ds(pl.multiple_of(k * 8, 8), 8), :], select_f)
        y = scale * y + gain * xf[pl.ds(at, Q), :]
        if early:
            out_ref[pl.ds(at, Q), :] = (y + back[pl.ds(at, Q), :].astype(F32)).astype(BF16)
        else:
            yf[pl.ds(at, Q), :] = y
        return e * (entering + uf[k])

    def finish_reverse(k, state):
        at = pl.multiple_of(k * Q, Q)
        e = exr[pl.ds(k, 1), :]
        entering = e * state
        y = dot(gcr[pl.ds(at, Q), :], jnp.concatenate([xsr[k], entering.astype(BF16)], axis=0))
        scale = spread(er[pl.ds(pl.multiple_of(k * 8, 8), 8), :], select_f)
        return (scale * y + gain * xr[pl.ds(at, Q), :]).astype(BF16), e * (entering + ur[k])

    def finish_early(i, state):
        k = chunks - 1 - i
        back[pl.ds(pl.multiple_of(k * Q, Q), Q), :], state = finish_reverse(k, state)
        return state

    late = TAIL * each

    lax.fori_loop(0, chunks // 4 - 1, by(4, step_mate), 0)
    arrive_halos()
    lax.fori_loop(chunks // 4 - 1, chunks // 4, by(4, step_mate), 0)
    reverse_total()
    states_out(1)
    lax.fori_loop(0, chunks // 4, by(4, step_forward), 0)
    tot_f[...] = lax.fori_loop(0, chunks // 4, by(4, forward_total), jnp.zeros((Q, width), F32))
    states_out(0)
    lax.fori_loop(0, chunks // 4, by(4, step_maps), 0)
    everyone = dall.at[pl.ds(0, seqs - 1)]
    pltpu.make_async_copy(everyone, everyone, d_recv).wait()
    states_back(1)
    lax.fori_loop(6, PIECES, push, 0)
    half = steps_of(own8, mate * HEADS + local, 0, er, fr)
    exr[...] = chunk_decay(half, 0)
    halos[4].wait_recv()

    @pl.when(here == seqs - 1)
    def _():
        pm[pl.ds(rows + EDGE, EDGE), :] = jnp.zeros((EDGE, width), BF16)

    pieces(0, PIECES // 2)
    states_back(0)
    pieces(PIECES // 2, PIECES - TAIL)
    state = lax.fori_loop(0, (chunks - late) // 4, by(4, finish_early), entered())
    others(inc_f, b_recv.at[0])
    forward = lax.fori_loop(0, late // 4, by(4, lambda k, st: finish_forward(k, st, False)), in_f[...])
    lax.fori_loop(late // 4, chunks // 4, by(4, lambda k, st: finish_forward(k, st, True)), forward)

    def finish_late(i, state):
        p = TAIL - 1 - i
        piece(p).wait_recv()
        ks = [p * each + each - 1 - j for j in range(each)]
        for k in ks:
            step_reverse(k)
        for k in ks:
            at = pl.multiple_of(k * Q, Q)
            rounded, state = finish_reverse(k, state)
            out_ref[pl.ds(at, Q), :] = (yf[pl.ds(at, Q), :] + rounded.astype(F32)).astype(BF16)
        return state

    lax.fori_loop(0, TAIL, finish_late, state)

    for copy in halos:
        copy.wait_send()

    for p in range(PIECES):
        piece(p).wait_send()

    pltpu.make_async_copy(everyone, everyone, d_send).wait()
    for way in (0, 1):
        others(got[way], a_send.at[way])
        others(inc[way], b_send.at[way], seqs - 1 + way)


def per_device(inputs, bc_inputs, dt_raw, conv_inner, conv_state, log_rate, dt_bias, skip_gain):
    seqs, ways = lax.axis_size("seq"), lax.axis_size("head")
    rows, width = inputs.shape
    chunks, share, wing = rows // Q, Q // seqs, width // 2
    anywhere = pl.BlockSpec(memory_space=pl.ANY)
    vmem = pl.BlockSpec(memory_space=pltpu.VMEM)
    padded = pltpu.VMEM((rows + 2 * EDGE, width), BF16)
    steps, decays = pltpu.VMEM((chunks * 8, Q), F32), pltpu.VMEM((chunks, width), F32)
    dma = pltpu.SemaphoreType.DMA
    return pl.pallas_call(
        functools.partial(kernel, seqs, ways),
        out_shape=jax.ShapeDtypeStruct((rows, width), BF16),
        in_specs=[anywhere] * 8,
        out_specs=vmem,
        scratch_shapes=[
            pltpu.VMEM(conv_state.shape, F32), pltpu.VMEM((1, log_rate.shape[0]), F32),
            pltpu.VMEM((1, log_rate.shape[0]), F32), pltpu.VMEM((1, log_rate.shape[0]), F32),
            pltpu.VMEM(dt_raw.shape, BF16), pltpu.VMEM((4, width), F32), pltpu.VMEM((4, width), F32),
            padded, padded, padded,
            pltpu.VMEM((rows, 2 * Q), BF16), pltpu.VMEM((rows, 2 * Q), BF16),
            pltpu.VMEM((rows, Q), BF16), pltpu.VMEM((rows, Q), BF16),
            pltpu.VMEM((chunks, Q, width), BF16), pltpu.VMEM((chunks, Q, width), BF16),
            pltpu.VMEM((rows, width), F32), pltpu.VMEM((rows, width), F32),
            pltpu.VMEM((chunks, Q, width), F32), pltpu.VMEM((chunks, Q, width), F32),
            pltpu.VMEM((rows, width), F32),
            steps, steps, steps, steps, decays, decays, decays,
            pltpu.VMEM((rows, width), BF16), pltpu.VMEM((Q, width), F32), pltpu.VMEM((Q, width), F32),
            pltpu.VMEM((seqs, share, width), F32), pltpu.VMEM((seqs, share, width), F32),
            pltpu.VMEM((seqs, share, width), F32), pltpu.VMEM((seqs, 2 * share, wing), BF16),
            pltpu.VMEM((Q, width), F32), pltpu.VMEM((seqs, 2 * share, wing), BF16),
            pltpu.VMEM((8, Q), F32), pltpu.VMEM((seqs, 8, Q), F32),
            dma((9,)), dma((5,)), dma((5,)), dma((PIECES,)), dma((PIECES,)),
            dma, dma, dma((2,)), dma((2,)), dma((2,)), dma((2,)),
        ],
        compiler_params=pltpu.CompilerParams(
            collective_id=0, has_side_effects=True, vmem_limit_bytes=60 * 2**20
        ),
    )(
        inputs, bc_inputs, dt_raw, conv_inner, conv_state,
        log_rate[None, :], dt_bias[None, :], skip_gain[None, :],
    )


def solution(mesh):
    return jax.shard_map(
        per_device,
        mesh=mesh,
        in_specs=(P("seq", "head"), P("seq", None), P(None, "seq"), P(), P(), P(), P(), P()),
        out_specs=P("seq", "head"),
        check_vma=False,
    )
```
